32 devices in a mesh: sp: 8 (over z, x), ch: 4 (over y, core).
Axes of the slice: x: 2, y: 2, z: 4, core: 2. Of those that a mesh axis runs over, the one named last changes fastest.
Arguments:
- field: bfloat16 [96, 180, 768], P('sp', None, 'ch'), may hold values from -150 to 150
- cotangent: bfloat16 [96, 180, 768], P('sp', None, 'ch'), may hold values from -6 to 6
- first_weight: float32 [2, 8, 96, 96], P(None, 'ch'), may hold values from -0.4375 to 0.4375
- first_bias: float32 [2, 8, 96], P(None, 'ch'), may hold values from -3 to 3
- second_weight: float32 [2, 8, 96, 96], P(None, 'ch'), may hold values from -0.4375 to 0.4375
- dense_in: bfloat16 [768, 1536], P(None, 'ch'), may hold values from -0.21875 to 0.21875
- dense_out: bfloat16 [1536, 768], P('ch'), may hold values from -0.15625 to 0.15625
Outputs:
- field_grad: bfloat16 [96, 180, 768], P('sp', None, 'ch')
- first_weight_grad: float32 [2, 8, 96, 96], P(None, 'ch')
- first_bias_grad: float32 [2, 8, 96], P(None, 'ch')
- second_weight_grad: float32 [2, 8, 96, 96], P(None, 'ch')
- dense_in_grad: bfloat16 [768, 1536], P(None, 'ch')
- dense_out_grad: bfloat16 [1536, 768], P('ch')
The draws below stay inside these ranges and needn't reach their ends.
All inputs are finite; a program needn't handle non-finite values.
Results may differ from the reference program's by a relative error of at most 0.0075.
Values may be sent and summed in bfloat16 or wider, within the bound.
No kernel may reach another device: no remote copies, remote signals or barrier semaphores. Data moves between devices by JAX's collectives and lax.ppermute only.
A program may use at most 128 MiB of HBM per device.

```python
import jax
import jax.numpy as jnp
from jax import lax

LAT = 90
LON = 180
NB = 8
BS = 96
HID = 1536
D = 768
SAMPLES = 1
LATP = 96


def draw_field(key, part):
    key = jax.random.fold_in(key, 11)
    subkeys = jax.random.split(key, 4)
    rows = SAMPLES * LATP
    base = jnp.clip(jax.random.normal(subkeys[0], (rows, LON, D), jnp.float32), -4.5, 4.5)
    rising = jnp.exp(jnp.linspace(0.0, 1.1, D))
    rough = jnp.exp(jax.random.uniform(subkeys[1], (D,), jnp.float32, -0.6, 0.6))
    offset = jnp.clip(jax.random.normal(subkeys[2], (D,), jnp.float32), -2.5, 2.5)
    cell_scale = jnp.exp(jax.random.uniform(subkeys[3], (rows, LON, 1), jnp.float32, -0.69, 1.6))
    return ((base * (rising * rough) + offset) * cell_scale).astype(jnp.bfloat16)


def levels(key, shape, cuts, least, top_value):
    level, own = 1.0, jax.random.fold_in(key, 6)
    for axis_at, shards_of in cuts:
        heights = jnp.exp(jax.random.uniform(jax.random.fold_in(own, axis_at), (shards_of,), jnp.float32, least / len(cuts), top_value / len(cuts)))
        level = level * jnp.repeat(heights, shape[axis_at] // shards_of).reshape([-1 if axis == axis_at else 1 for axis in range(len(shape))])
    return level


def centred(own_key, extent, deviation, reach, pieces=(), dtype=jnp.bfloat16):
    array = jax.random.normal(own_key, extent, jnp.float32) * deviation
    if len(pieces) > 0:
        array = levels(own_key, extent, pieces, -0.22, 0.18) * array
    return jnp.clip(array, min=-reach, max=reach).astype(dtype)


def setup_inputs(seed: int = 0) -> dict:
    splits = jax.random.split(jax.random.key(seed), 8)
    return {
        "field": draw_field(jax.random.fold_in(splits[7], 71), 0),
        "cotangent": centred(splits[1], (SAMPLES * LATP, LON, D), 1.0, 6.0, ((0, 8), (2, 4))),
        "first_weight": centred(splits[2], (2, NB, BS, BS), (2 * BS) ** -0.5, 0.4375, ((1, 4),), jnp.float32),
        "first_bias": centred(splits[3], (2, NB, BS), 0.5, 3.0, ((1, 4),), jnp.float32),
        "second_weight": centred(splits[4], (2, NB, BS, BS), (2 * BS) ** -0.5, 0.4375, ((1, 4),), jnp.float32),
        "dense_in": centred(splits[5], (D, HID), D ** -0.5, 0.21875, ((1, 4),)),
        "dense_out": centred(splits[6], (HID, D), HID ** -0.5, 0.15625, ((0, 4),)),
    }


eps = 1e-05
highest = lax.Precision.HIGHEST

def exact_gelu(values):
    return jax.nn.gelu(values, approximate=False)

def block_mixing(spec_real, spec_imag, first_weight, first_bias, second_weight):

    def mult(values, matrix):
        return jnp.einsum('hkbi,bio->hkbo', values, matrix, precision=highest)
    pre_real = mult(spec_real, first_weight[0]) - mult(spec_imag, first_weight[1]) + first_bias[0]
    pre_imag = mult(spec_imag, first_weight[0]) + mult(spec_real, first_weight[1]) + first_bias[1]
    act_real = exact_gelu(pre_real)
    act_imag = exact_gelu(pre_imag)
    out_real = mult(act_real, second_weight[0]) - mult(act_imag, second_weight[1])
    out_imag = mult(act_imag, second_weight[0]) + mult(act_real, second_weight[1])
    return (out_real, out_imag)

def spectral_filter(normed, first_weight, first_bias, second_weight):
    spectrum = jnp.fft.rfft2(normed, axes=(0, 1), norm='ortho')
    shape = (LAT, LON // 2 + 1, NB, BS)
    out_real, out_imag = block_mixing(jnp.real(spectrum).reshape(shape), jnp.imag(spectrum).reshape(shape), first_weight, first_bias, second_weight)
    mixed = (out_real + 1j * out_imag).reshape(LAT, LON // 2 + 1, NB * BS)
    return jnp.fft.irfft2(mixed, s=(LAT, LON), axes=(0, 1), norm='ortho')

def normalize(values):
    center = lax.optimization_barrier(jnp.mean(values, axis=-1, keepdims=True))
    centered = values - center
    spread = lax.optimization_barrier(jnp.mean(centered * centered, axis=-1, keepdims=True))
    recip = lax.rsqrt(spread + eps)
    return (centered * recip, recip)

def norm_back(normed, recip, incoming):
    first = lax.optimization_barrier(jnp.mean(incoming, axis=-1, keepdims=True))
    second = lax.optimization_barrier(jnp.mean(incoming * normed, axis=-1, keepdims=True))
    return recip * (incoming - first - normed * second)

def one_sample(field, cotangent, first_weight, first_bias, second_weight, dense_in, dense_out):
    inputs = field[:LAT].astype(jnp.float32)
    upstream = cotangent[:LAT]
    normed_in, recip_in = normalize(inputs)
    filtered, filter_back = jax.vjp(spectral_filter, normed_in, first_weight, first_bias, second_weight)
    summed = inputs + normed_in + filtered
    normed_sum, recip_sum = normalize(summed)
    normed_mid = normed_sum.astype(jnp.bfloat16)
    flat_mid = normed_mid.reshape(LAT * LON, NB * BS)
    flat_up = upstream.reshape(LAT * LON, NB * BS)
    hidden_pre = jnp.dot(flat_mid, dense_in, preferred_element_type=jnp.float32)
    hidden_act = exact_gelu(hidden_pre).astype(jnp.bfloat16)
    hidden_in = jnp.dot(flat_up, dense_out.T, preferred_element_type=jnp.float32)
    gelu_value, gelu_back = jax.vjp(exact_gelu, hidden_pre)
    hidden_grad = gelu_back(hidden_in)[0].astype(jnp.bfloat16)
    mid_grad = jnp.dot(hidden_grad, dense_in.T, preferred_element_type=jnp.float32)
    dense_in_grad = jnp.dot(flat_mid.T, hidden_grad, preferred_element_type=jnp.float32)
    dense_out_grad = jnp.dot(hidden_act.T, flat_up, preferred_element_type=jnp.float32)
    summed_grad = upstream.astype(jnp.float32) + norm_back(normed_sum, recip_sum, mid_grad.reshape(LAT, LON, NB * BS))
    spectral_grad, first_weight_grad, first_bias_grad, second_weight_grad = filter_back(summed_grad)
    normed_grad = summed_grad + spectral_grad
    field_grad = (summed_grad + norm_back(normed_in, recip_in, normed_grad)).astype(jnp.bfloat16)
    padding = jnp.zeros((LATP - LAT, LON, NB * BS), jnp.bfloat16)
    field_grad = jnp.concatenate([field_grad, padding], axis=0)
    return (field_grad, first_weight_grad, first_bias_grad, second_weight_grad, dense_in_grad, dense_out_grad)

def reference(field, cotangent, first_weight, first_bias, second_weight, dense_in, dense_out):
    fields = field.reshape(SAMPLES, LATP, LON, NB * BS)
    cotangents = cotangent.reshape(SAMPLES, LATP, LON, NB * BS)

    def run(pair):
        return one_sample(pair[0], pair[1], first_weight, first_bias, second_weight, dense_in, dense_out)
    field_grads, fw_grads, fb_grads, sw_grads, in_grads, out_grads = lax.map(run, (fields, cotangents))
    field_grad = field_grads.reshape(SAMPLES * LATP, LON, NB * BS)
    dense_in_grad = lax.optimization_barrier(jnp.sum(in_grads, axis=0)).astype(jnp.bfloat16)
    dense_out_grad = lax.optimization_barrier(jnp.sum(out_grads, axis=0)).astype(jnp.bfloat16)
    return (field_grad, lax.optimization_barrier(jnp.sum(fw_grads, axis=0)), lax.optimization_barrier(jnp.sum(fb_grads, axis=0)), lax.optimization_barrier(jnp.sum(sw_grads, axis=0)), dense_in_grad, dense_out_grad)
```

```python
import math

import jax
import jax.numpy as jnp
import numpy as np
from jax import lax
from jax.experimental import pallas as pl
from jax.experimental.pallas import tpu as pltpu
from jax.sharding import PartitionSpec as P

LAT = 90
BAND_MAX = 16
LANES = 128
HALF = 64

eps = 1e-05
f32 = jnp.float32
bf16 = jnp.bfloat16
high = lax.Precision.HIGH
VMEM_BYTES = 50 * 2**20


def up_to(value, step):
    return (value + step - 1) // step * step


class Sizes:
    def __init__(self, block, n_sp, n_ch):
        self.rows, self.lon, self.chans = block
        self.n_sp, self.n_ch = n_sp, n_ch
        self.width = self.chans * n_ch
        self.own = -(-self.rows // n_ch)
        self.bands = min(BAND_MAX, n_sp)
        self.samples = n_sp // self.bands
        self.modes = -(-(self.lon // 2 + 1) // n_sp)
        self.all_modes = self.modes * n_sp
        self.parts = 2 * self.chans // LANES
        self.pad = up_to(self.parts * self.own * self.modes, 16)
        self.sources = self.bands * n_ch
        self.lat_in = self.own * self.sources
        self.lat_modes = up_to(LAT, 16)
        self.planes = self.samples * self.modes
        self.lon_pad = up_to(self.lon, 16)

    def slot(self, q, r, m):
        return (q * self.own + r) * self.modes + m


def lon_tables(sz):
    mode = (np.arange(sz.n_sp)[None, :] * sz.modes + np.arange(sz.modes)[:, None]).reshape(-1, 1)
    cell = np.arange(sz.lon)[None, :]
    phase = 2.0 * np.pi / sz.lon * (mode * cell % sz.lon)
    live = (mode <= sz.lon // 2).astype(np.float64)
    inner = ((mode > 0) & (mode < sz.lon // 2)).astype(np.float64)
    scale = 1.0 / math.sqrt(sz.lon)
    cosine = np.cos(phase) * live * scale
    sine = np.sin(phase) * inner * scale
    forward = np.concatenate([cosine, -sine], axis=0)
    inverse = np.concatenate([cosine * (live + inner), -2.0 * sine], axis=0).T
    return forward.astype(np.float32), np.ascontiguousarray(inverse).astype(np.float32)


def lat_table(sz):
    r = np.arange(sz.own)[:, None, None]
    band = np.arange(sz.bands)[None, :, None]
    c = np.arange(sz.n_ch)[None, None, :]
    cell = band * sz.rows + c * sz.own + r
    live = np.logical_and(c * sz.own + r < sz.rows, cell < LAT).reshape(1, -1)
    cell = cell.reshape(1, -1)
    mode = np.arange(sz.lat_modes)[:, None]
    live = np.logical_and(live, mode < LAT) / math.sqrt(LAT)
    phase = 2.0 * np.pi / LAT * (mode * cell % LAT)
    return (
        (np.cos(phase) * live).astype(np.float32),
        (np.sin(phase) * live).astype(np.float32),
    )


def gelu_pair(v):
    cdf = 0.5 * (1.0 + lax.erf(v * np.float32(math.sqrt(0.5))))
    pdf = jnp.exp(-0.5 * v * v) * np.float32(1.0 / math.sqrt(2.0 * math.pi))
    return v * cdf, cdf + v * pdf


def mm(a, b, precision=high):
    return jnp.dot(a, b, precision=precision, preferred_element_type=f32)


def swap(values):
    lane = lax.broadcasted_iota(jnp.int32, values.shape, 1)
    turned = pltpu.roll(values, HALF, 1)
    return jnp.where(lane < HALF, turned, -turned)


def store_modes(sz, scr, y, r, c):
    n = sz.all_modes
    re, im = y[:n], y[n:]
    pieces = (re[:, :LANES], im[:, :LANES], re[:, LANES:] + pltpu.roll(im[:, LANES:], HALF, 1))
    for q, piece in enumerate(pieces):
        for m in range(sz.modes):
            scr[pl.ds(c * sz.pad + sz.slot(q, r, m), sz.n_sp, stride=sz.n_ch * sz.pad), :] = piece[
                m * sz.n_sp : (m + 1) * sz.n_sp
            ]


def load_modes(sz, scr, r, c):
    q0, q1, q2 = (
        jnp.concatenate(
            [
                scr[pl.ds(c * sz.pad + sz.slot(q, r, m), sz.n_sp, stride=sz.n_ch * sz.pad), :]
                for m in range(sz.modes)
            ],
            axis=0,
        )
        for q in range(3)
    )
    left = jnp.concatenate([q0, q1], axis=0)
    right = jnp.concatenate([q2, pltpu.roll(q2, HALF, 1)], axis=0)
    return jnp.concatenate([left, right], axis=1)


def wide(values):
    rows, lanes = values.shape
    return jnp.concatenate([values, jnp.zeros((rows, up_to(lanes, LANES) - lanes), f32)], axis=1)


def plane_start(sz, s, q, r, m):
    return s * sz.sources * sz.pad + sz.slot(q, r, m)


def center_scale(chunks, width):
    mean = sum(jnp.sum(v, axis=-1, keepdims=True) for v in chunks) / width
    chunks = [v - mean for v in chunks]
    var = sum(jnp.sum(v * v, axis=-1, keepdims=True) for v in chunks) / width
    recip = lax.rsqrt(var + eps)
    return [v * recip for v in chunks], recip


def norm_back(normed, recip, incoming, width):
    first = sum(jnp.sum(g, axis=-1, keepdims=True) for g in incoming) / width
    second = sum(jnp.sum(g * z, axis=-1, keepdims=True) for g, z in zip(incoming, normed)) / width
    return [recip * (g - first - z * second) for g, z in zip(incoming, normed)]


def norm_spectrum_kernel(sz, x_ref, tab_ref, out_ref, scr):
    for r in range(sz.own):
        normed, _ = center_scale([x_ref[c, r].astype(f32) for c in range(sz.n_ch)], sz.width)
        for c in range(sz.n_ch):
            store_modes(sz, scr, mm(tab_ref[...], wide(normed[c])), r, c)
    out_ref[...] = scr[...].astype(bf16)


def lat_forward(sz, scr, cs, p):
    s, m = divmod(p, sz.modes)
    x0, x1, x2 = (
        jnp.concatenate(
            [
                scr[pl.ds(plane_start(sz, s, q, r, m), sz.sources, stride=sz.pad), :]
                for r in range(sz.own)
            ],
            axis=0,
        )
        for q in range(3)
    )
    both = jnp.concatenate(
        [jnp.concatenate([x0, x1, x2], axis=1), jnp.concatenate([x1, -x0, swap(x2)], axis=1)], axis=0
    )
    return mm(cs, both)


def lat_inverse(sz, scr, cs_t, o, p):
    s, m = divmod(p, sz.modes)
    o0, o1, o2 = (o[:, q * LANES : (q + 1) * LANES] for q in range(3))
    both = jnp.concatenate(
        [jnp.concatenate([o0, o1, o2], axis=1), jnp.concatenate([-o1, o0, -swap(o2)], axis=1)], axis=0
    )
    y = mm(cs_t, both)
    for q in range(3):
        for r in range(sz.own):
            scr[pl.ds(plane_start(sz, s, q, r, m), sz.sources, stride=sz.pad), :] = y[
                r * sz.sources : (r + 1) * sz.sources, q * LANES : (q + 1) * LANES
            ]


def mix_kernel(sz, in_ref, cs_ref, cst_ref, w1_ref, b1_ref, w2_ref,
               out_ref, spec_ref, act_ref, slope_ref, scr, mixed):
    n = sz.lat_modes
    scr[...] = in_ref[...].astype(f32)
    for p in range(sz.planes):
        spec_ref[p * n : (p + 1) * n, :] = lat_forward(sz, scr, cs_ref[...], p)

    def block(i, carry):
        rows = pl.ds(pl.multiple_of(i * 2 * n, 16), 2 * n)
        act, slope = gelu_pair(mm(spec_ref[rows, :], w1_ref[...]) + b1_ref[...])
        act_ref[rows, :] = act
        slope_ref[rows, :] = slope
        mixed[rows, :] = mm(act, w2_ref[...])
        return carry

    lax.fori_loop(0, sz.planes // 2, block, 0)
    for p in range(sz.planes):
        lat_inverse(sz, scr, cst_ref[...], mixed[p * n : (p + 1) * n, :], p)
    out_ref[...] = scr[...].astype(bf16)


def mix_back_kernel(sz, in_ref, cs_ref, cst_ref, w1t_ref, w2t_ref, slope_ref,
                    out_ref, dmix_ref, dpre_ref, scr, dspec):
    n = sz.lat_modes
    scr[...] = in_ref[...].astype(f32)
    for p in range(sz.planes):
        dmix_ref[p * n : (p + 1) * n, :] = lat_forward(sz, scr, cs_ref[...], p)

    def block(i, carry):
        rows = pl.ds(pl.multiple_of(i * 2 * n, 16), 2 * n)
        dpre = mm(dmix_ref[rows, :], w2t_ref[...]) * slope_ref[rows, :]
        dpre_ref[rows, :] = dpre
        dspec[rows, :] = mm(dpre, w1t_ref[...])
        return carry

    lax.fori_loop(0, sz.planes // 2, block, 0)
    for p in range(sz.planes):
        lat_inverse(sz, scr, cst_ref[...], dspec[p * n : (p + 1) * n, :], p)
    out_ref[...] = scr[...].astype(bf16)


def mlp_kernel(sz, in_ref, x_ref, up_ref, inv_ref, invt_ref, win_ref, wout_ref,
               out_ref, sg_ref, mid_ref, upf_ref, act_ref, hg_ref, scr, z_scr, mg_scr, rs_scr):
    scr[...] = in_ref[...].astype(f32)
    mid_ref[...] = jnp.zeros(mid_ref.shape, bf16)
    upf_ref[...] = jnp.zeros(upf_ref.shape, bf16)
    c_all = range(sz.n_ch)

    def place(r, c):
        return (slice(r * sz.lon_pad, r * sz.lon_pad + sz.lon), slice(c * sz.chans, (c + 1) * sz.chans))

    for r in range(sz.own):
        xs = [x_ref[c, r].astype(f32) for c in c_all]
        normed, _ = center_scale(xs, sz.width)
        summed = [
            xs[c] + normed[c] + mm(inv_ref[...], load_modes(sz, scr, r, c))[:, : sz.chans] for c in c_all
        ]
        zs, recip = center_scale(summed, sz.width)
        rs_scr[r] = jnp.broadcast_to(recip, (sz.lon, LANES))
        for c in c_all:
            z_scr[c, r] = zs[c]
            mid_ref[place(r, c)] = zs[c].astype(bf16)
            upf_ref[place(r, c)] = up_ref[c, r]
    mg_scr[...] = jnp.zeros(mg_scr.shape, f32)
    nt = (((1,), (1,)), ((), ()))

    def hidden(j, carry):
        pre = mm(mid_ref[...], win_ref[j], None)
        back = lax.dot_general(upf_ref[...], wout_ref[j], nt, preferred_element_type=f32)
        act, slope = gelu_pair(pre)
        act_ref[j] = act.astype(bf16)
        grad = (back * slope).astype(bf16)
        hg_ref[j] = grad
        mg_scr[...] += lax.dot_general(grad, win_ref[j], nt, preferred_element_type=f32)
        return carry

    lax.fori_loop(0, sz.n_ch, hidden, 0)
    for r in range(sz.own):
        zs = [z_scr[c, r] for c in c_all]
        grads = norm_back(zs, rs_scr[r][:, :1], [mg_scr[place(r, c)] for c in c_all], sz.width)
        for c in c_all:
            total = up_ref[c, r].astype(f32) + grads[c]
            sg_ref[c, r] = total
            store_modes(sz, scr, mm(invt_ref[...], wide(total)), r, c)
    out_ref[...] = scr[...].astype(bf16)


def field_kernel(sz, in_ref, x_ref, sg_ref, fwdt_ref, out_ref, scr):
    scr[...] = in_ref[...].astype(f32)
    c_all = range(sz.n_ch)
    for r in range(sz.own):
        normed, recip = center_scale([x_ref[c, r].astype(f32) for c in c_all], sz.width)
        sg = [sg_ref[c, r] for c in c_all]
        incoming = [sg[c] + mm(fwdt_ref[...], load_modes(sz, scr, r, c))[:, : sz.chans] for c in c_all]
        grads = norm_back(normed, recip, incoming, sz.width)
        for c in c_all:
            out_ref[c, r] = (sg[c] + grads[c]).astype(bf16)


def call(body, outs, scratch, args, flops):
    return pl.pallas_call(
        body,
        out_shape=outs,
        scratch_shapes=scratch,
        compiler_params=pltpu.CompilerParams(vmem_limit_bytes=VMEM_BYTES),
        cost_estimate=pl.CostEstimate(flops=flops, bytes_accessed=8 * 2**20, transcendentals=0),
    )(*args)


def block_diagonal(weight):
    blocks, size = weight.shape[0], weight.shape[1]
    ident = jnp.eye(blocks, dtype=f32)
    return jnp.einsum("be,bio->bieo", ident, weight).reshape(blocks * size, blocks * size)


def lane_order(values, axis, chans):
    def cut(a, b):
        return lax.slice_in_dim(values, a, b, axis=axis)
    return jnp.concatenate(
        [cut(0, LANES), cut(chans, chans + LANES), cut(LANES, chans), cut(chans + LANES, 2 * chans)], axis=axis
    )


def natural_order(values, axis, chans):
    def cut(a, b):
        return lax.slice_in_dim(values, a, b, axis=axis)
    rest = chans - LANES
    return jnp.concatenate(
        [cut(0, LANES), cut(2 * LANES, 2 * LANES + rest), cut(LANES, 2 * LANES), cut(2 * LANES + rest, 2 * chans)],
        axis=axis,
    )


def big_weight(weight):
    real, imag = block_diagonal(weight[0]), block_diagonal(weight[1])
    full = jnp.concatenate(
        [jnp.concatenate([real, imag], axis=1), jnp.concatenate([-imag, real], axis=1)], axis=0
    )
    chans = real.shape[0]
    return lane_order(lane_order(full, 0, chans), 1, chans)


def small_grad(big, blocks):
    chans = big.shape[0] // 2
    size = chans // blocks
    full = natural_order(natural_order(big, 0, chans), 1, chans)
    full = full.reshape(2, blocks, size, 2, blocks, size)
    diag = jnp.stack([full[:, b, :, :, b, :] for b in range(blocks)], axis=0)
    real = diag[:, 0, :, 0] + diag[:, 1, :, 1]
    imag = diag[:, 0, :, 1] - diag[:, 1, :, 0]
    return jnp.stack([real, imag], axis=0)


def exchange(axis, bit, values):
    n = lax.axis_size(axis)
    return lax.ppermute(values, axis, [(i, i ^ bit) for i in range(n)])


def halve(axis, bit, values):
    mine = (lax.axis_index(axis) // bit) % 2
    kept = lax.dynamic_index_in_dim(values, mine, 0, keepdims=False)
    sent = lax.dynamic_index_in_dim(values, 1 - mine, 0, keepdims=False).astype(bf16)
    return kept + exchange(axis, bit, sent).astype(f32)


def double(axis, bit, values):
    mine = (lax.axis_index(axis) // bit) % 2
    other = exchange(axis, bit, values)
    first = jnp.where(mine == 0, values, other)
    second = jnp.where(mine == 0, other, values)
    return jnp.stack([first, second], axis=0)


def bits(n):
    return [1 << i for i in range(n.bit_length() - 1)]


def dense_sums(partial, n_sp, n_ch):
    values = partial
    _, rows, width = partial.shape
    for bit in bits(n_ch):
        left = values.shape[0] // 2
        values = halve("ch", bit, values.reshape(left, 2, rows, width).swapaxes(0, 1))
    values = values.reshape(rows, width)
    for bit in bits(n_sp):
        values = halve("sp", bit, values.reshape(2, values.shape[0] // 2, width))
    values = values.astype(bf16)
    for bit in reversed(bits(n_sp)):
        values = double("sp", bit, values).reshape(-1, width)
    return values


def local(field, cotangent, first_weight, first_bias, second_weight, dense_in, dense_out):
    n_sp, n_ch = lax.axis_size("sp"), lax.axis_size("ch")
    sz = Sizes(field.shape, n_sp, n_ch)
    blocks = first_weight.shape[1]
    both = ("sp", "ch")
    hid = dense_in.shape[1]
    forward, inverse = (jnp.asarray(t) for t in lon_tables(sz))
    cosine, sine = lat_table(sz)
    cs = jnp.asarray(np.concatenate([cosine, sine], axis=1))
    cs_t = jnp.asarray(np.concatenate([cosine.T, sine.T], axis=1))

    def to_cells(values):
        extra = sz.own * n_ch - sz.rows
        if extra:
            values = jnp.pad(values, ((0, extra), (0, 0), (0, 0)))
        values = values.reshape(n_ch, sz.own, sz.lon, sz.chans)
        return lax.all_to_all(values, "ch", split_axis=0, concat_axis=0, tiled=True)

    def swap_modes(message):
        message = message.reshape(n_sp * n_ch, sz.pad, LANES)
        message = lax.all_to_all(message, both, split_axis=0, concat_axis=0, tiled=True)
        return message.reshape(n_sp * n_ch * sz.pad, LANES)

    row_index = lax.axis_index("sp") % sz.bands * sz.rows + jnp.arange(sz.rows)
    valid = (row_index < LAT)[:, None, None]
    x = to_cells(field)
    up = to_cells(jnp.where(valid, cotangent, jnp.zeros_like(cotangent)))
    win = lax.all_gather(dense_in, "ch", axis=0)
    wout = lax.all_gather(dense_out, "ch", axis=0)
    w1, w2 = big_weight(first_weight), big_weight(second_weight)
    b1 = lane_order(first_bias.reshape(1, -1), 1, sz.chans)

    message = jax.ShapeDtypeStruct((n_sp * n_ch * sz.pad, LANES), bf16)
    scr = pltpu.VMEM(message.shape, f32)
    flat = jax.ShapeDtypeStruct((sz.planes * sz.lat_modes, 2 * sz.chans), f32)
    flat_scr = pltpu.VMEM(flat.shape, f32)
    cells = (n_ch, sz.own, sz.lon, sz.chans)

    def bind(kernel):
        return lambda *refs: kernel(sz, *refs)

    sent = call(bind(norm_spectrum_kernel), message, [scr], (x, forward), 10**9)
    got = swap_modes(sent)
    sent, spec, act, slope = call(
        bind(mix_kernel), (message, flat, flat, flat), [scr, flat_scr], (got, cs, cs_t, w1, b1, w2), 4 * 10**9
    )
    got = swap_modes(sent)
    tokens = sz.own * sz.lon_pad
    grown = jax.ShapeDtypeStruct((tokens, sz.width), bf16)
    hidden = jax.ShapeDtypeStruct((n_ch, tokens, hid), bf16)
    sent, sg, mid, upf, hidden_act, hidden_grad = call(
        bind(mlp_kernel),
        (message, jax.ShapeDtypeStruct(cells, f32), grown, grown, hidden, hidden),
        [scr, pltpu.VMEM(cells, f32), pltpu.VMEM(grown.shape, f32), pltpu.VMEM((sz.own, sz.lon, LANES), f32)],
        (got, x, up, inverse, inverse.T, win, wout),
        10**10,
    )
    got = swap_modes(sent)
    in_part = jnp.einsum("jth,td->jhd", hidden_grad, mid, preferred_element_type=f32)
    out_part = jnp.einsum("jth,td->jhd", hidden_act, upf, preferred_element_type=f32)
    dense = dense_sums(jnp.concatenate([in_part, out_part], axis=1), n_sp, n_ch)
    sent, dmix, dpre = call(
        bind(mix_back_kernel), (message, flat, flat), [scr, flat_scr], (got, cs, cs_t, w1.T, w2.T, slope), 4 * 10**9
    )
    got = swap_modes(sent)
    tn = (((0,), (0,)), ((), ()))
    w1_grad = small_grad(lax.dot_general(spec, dpre, tn, precision=high, preferred_element_type=f32), blocks)
    w2_grad = small_grad(lax.dot_general(act, dmix, tn, precision=high, preferred_element_type=f32), blocks)
    b1_grad = natural_order(jnp.sum(dpre, axis=0, keepdims=True), 1, sz.chans).reshape(first_bias.shape)
    w1_grad, w2_grad, b1_grad = lax.psum((w1_grad, w2_grad, b1_grad), "sp")
    grad = call(bind(field_kernel), jax.ShapeDtypeStruct(cells, bf16), [scr], (got, x, sg, forward.T), 10**9)
    grad = lax.all_to_all(grad, "ch", split_axis=0, concat_axis=0, tiled=True)
    grad = grad.reshape(n_ch * sz.own, sz.lon, sz.chans)[: sz.rows]
    return (grad, w1_grad, b1_grad, w2_grad, dense[:hid].T, dense[hid:])


def solution(mesh):
    placed = (
        P("sp", None, "ch"),
        P("sp", None, "ch"),
        P(None, "ch", None, None),
        P(None, "ch", None),
        P(None, "ch", None, None),
        P(None, "ch"),
        P("ch", None),
    )
    return jax.shard_map(
        local,
        mesh=mesh,
        in_specs=placed,
        out_specs=(
            P("sp", None, "ch"),
            P(None, "ch", None, None),
            P(None, "ch", None),
            P(None, "ch", None, None),
            P(None, "ch"),
            P("ch", None),
        ),
        check_vma=False,
    )
```

```python
import math

import jax
import jax.numpy as jnp
import numpy as np
from jax import lax
from jax.experimental import pallas as pl
from jax.experimental.pallas import tpu as pltpu
from jax.sharding import PartitionSpec as P

LAT = 90
BAND_MAX = 16
LANES = 128
HALF = 64

eps = 1e-05
f32 = jnp.float32
bf16 = jnp.bfloat16
HIGH = lax.Precision.HIGH
VMEM_BYTES = 50 * 2**20


def up_to(value, step):
    return (value + step - 1) // step * step


class Sizes:
    def __init__(self, block, n_sp, n_ch):
        self.rows, self.lon, self.chans = block
        self.n_sp, self.n_ch = n_sp, n_ch
        self.width = self.chans * n_ch
        self.own = -(-self.rows // n_ch)
        self.bands = min(BAND_MAX, n_sp)
        self.samples = n_sp // self.bands
        self.modes = -(-(self.lon // 2 + 1) // n_sp)
        self.all_modes = self.modes * n_sp
        self.parts = 2 * self.chans // LANES
        self.pad = up_to(self.parts * self.own * self.modes, 16)
        self.sources = self.bands * n_ch
        self.lat_in = self.own * self.sources
        self.lat_modes = up_to(LAT, 16)
        self.planes = self.samples * self.modes
        self.lon_pad = up_to(self.lon, 16)

    def slot(self, q, r, m):
        return (q * self.own + r) * self.modes + m


def lon_tables(sz):
    mode = (np.arange(sz.n_sp)[None, :] * sz.modes + np.arange(sz.modes)[:, None]).reshape(-1, 1)
    cell = np.arange(sz.lon)[None, :]
    phase = 2.0 * np.pi / sz.lon * (mode * cell % sz.lon)
    live = (mode <= sz.lon // 2).astype(np.float64)
    inner = ((mode > 0) & (mode < sz.lon // 2)).astype(np.float64)
    scale = 1.0 / math.sqrt(sz.lon)
    cosine = np.cos(phase) * live * scale
    sine = np.sin(phase) * inner * scale
    forward = np.concatenate([cosine, -sine], axis=0)
    inverse = np.concatenate([cosine * (live + inner), -2.0 * sine], axis=0).T
    return forward.astype(np.float32), np.ascontiguousarray(inverse).astype(np.float32)


def lat_table(sz):
    r = np.arange(sz.own)[:, None, None]
    band = np.arange(sz.bands)[None, :, None]
    c = np.arange(sz.n_ch)[None, None, :]
    cell = band * sz.rows + c * sz.own + r
    live = np.logical_and(c * sz.own + r < sz.rows, cell < LAT).reshape(1, -1)
    cell = cell.reshape(1, -1)
    mode = np.arange(sz.lat_modes)[:, None]
    live = np.logical_and(live, mode < LAT) / math.sqrt(LAT)
    phase = 2.0 * np.pi / LAT * (mode * cell % LAT)
    return (
        (np.cos(phase) * live).astype(np.float32),
        (np.sin(phase) * live).astype(np.float32),
    )


def gelu_pair(v):
    cdf = 0.5 * (1.0 + lax.erf(v * np.float32(math.sqrt(0.5))))
    pdf = jnp.exp(-0.5 * v * v) * np.float32(1.0 / math.sqrt(2.0 * math.pi))
    return v * cdf, cdf + v * pdf


def mm(a, b, precision=HIGH):
    return jnp.dot(a, b, precision=precision, preferred_element_type=f32)


def swap(values):
    lane = lax.broadcasted_iota(jnp.int32, values.shape, 1)
    turned = pltpu.roll(values, HALF, 1)
    return jnp.where(lane < HALF, turned, -turned)


def store_modes(sz, scr, y, r, c):
    n = sz.all_modes
    re, im = y[:n], y[n:]
    pieces = (re[:, :LANES], im[:, :LANES], re[:, LANES:] + pltpu.roll(im[:, LANES:], HALF, 1))
    for q, piece in enumerate(pieces):
        for m in range(sz.modes):
            scr[pl.ds(c * sz.pad + sz.slot(q, r, m), sz.n_sp, stride=sz.n_ch * sz.pad), :] = piece[
                m * sz.n_sp : (m + 1) * sz.n_sp
            ]


def load_modes(sz, scr, r, c):
    q0, q1, q2 = (
        jnp.concatenate(
            [
                scr[pl.ds(c * sz.pad + sz.slot(q, r, m), sz.n_sp, stride=sz.n_ch * sz.pad), :]
                for m in range(sz.modes)
            ],
            axis=0,
        )
        for q in range(3)
    )
    left = jnp.concatenate([q0, q1], axis=0)
    right = jnp.concatenate([q2, pltpu.roll(q2, HALF, 1)], axis=0)
    return jnp.concatenate([left, right], axis=1)


def wide(values):
    rows, lanes = values.shape
    return jnp.concatenate([values, jnp.zeros((rows, up_to(lanes, LANES) - lanes), f32)], axis=1)


def plane_start(sz, s, q, r, m):
    return s * sz.sources * sz.pad + sz.slot(q, r, m)


def center_scale(chunks, width):
    mean = sum(jnp.sum(v, axis=-1, keepdims=True) for v in chunks) / width
    chunks = [v - mean for v in chunks]
    var = sum(jnp.sum(v * v, axis=-1, keepdims=True) for v in chunks) / width
    recip = lax.rsqrt(var + eps)
    return [v * recip for v in chunks], recip


def norm_back(normed, recip, incoming, width):
    first = sum(jnp.sum(g, axis=-1, keepdims=True) for g in incoming) / width
    second = sum(jnp.sum(g * z, axis=-1, keepdims=True) for g, z in zip(incoming, normed)) / width
    return [recip * (g - first - z * second) for g, z in zip(incoming, normed)]


def gather_parts(sz, at_ref, own_ref, parts, out_ref):
    me = at_ref[4]
    for r in range(sz.own):
        out_ref[me, r] = own_ref[me * sz.own + r]
    for d, part in enumerate(parts):
        out_ref[me ^ (d + 1)] = part[...]


def norm_spectrum_kernel(sz, at_ref, *refs):
    own_ref, *parts = refs[: sz.n_ch]
    tab_ref, out_ref, x_ref, scr = refs[sz.n_ch :]
    gather_parts(sz, at_ref, own_ref, parts, x_ref)
    for r in range(sz.own):
        normed, _ = center_scale([x_ref[c, r].astype(f32) for c in range(sz.n_ch)], sz.width)
        for c in range(sz.n_ch):
            store_modes(sz, scr, mm(tab_ref[...], wide(normed[c])), r, c)
    out_ref[...] = scr[...].astype(bf16)


def lat_forward(sz, scr, cs, p):
    s, m = divmod(p, sz.modes)
    x0, x1, x2 = (
        jnp.concatenate(
            [
                scr[pl.ds(plane_start(sz, s, q, r, m), sz.sources, stride=sz.pad), :]
                for r in range(sz.own)
            ],
            axis=0,
        )
        for q in range(3)
    )
    both = jnp.concatenate(
        [jnp.concatenate([x0, x1, x2], axis=1), jnp.concatenate([x1, -x0, swap(x2)], axis=1)], axis=0
    )
    return mm(cs, both)


def lat_inverse(sz, scr, cs_t, o, p):
    s, m = divmod(p, sz.modes)
    o0, o1, o2 = (o[:, q * LANES : (q + 1) * LANES] for q in range(3))
    both = jnp.concatenate(
        [jnp.concatenate([o0, o1, o2], axis=1), jnp.concatenate([-o1, o0, -swap(o2)], axis=1)], axis=0
    )
    y = mm(cs_t, both)
    for q in range(3):
        for r in range(sz.own):
            scr[pl.ds(plane_start(sz, s, q, r, m), sz.sources, stride=sz.pad), :] = y[
                r * sz.sources : (r + 1) * sz.sources, q * LANES : (q + 1) * LANES
            ]


def mix_kernel(sz, in_ref, cs_ref, cst_ref, w1_ref, b1_ref, w2_ref,
               out_ref, spec_ref, act_ref, slope_ref, scr, mixed):
    n = sz.lat_modes
    scr[...] = in_ref[...].astype(f32)
    for p in range(sz.planes):
        spec_ref[p * n : (p + 1) * n, :] = lat_forward(sz, scr, cs_ref[...], p)

    def block(i, carry):
        rows = pl.ds(pl.multiple_of(i * 2 * n, 16), 2 * n)
        act, slope = gelu_pair(mm(spec_ref[rows, :], w1_ref[...]) + b1_ref[...])
        act_ref[rows, :] = act
        slope_ref[rows, :] = slope
        mixed[rows, :] = mm(act, w2_ref[...])
        return carry

    lax.fori_loop(0, sz.planes // 2, block, 0)
    for p in range(sz.planes):
        lat_inverse(sz, scr, cst_ref[...], mixed[p * n : (p + 1) * n, :], p)
    out_ref[...] = scr[...].astype(bf16)


def mix_back_kernel(sz, in_ref, cs_ref, w2t_ref, slope_ref, dmix_ref, dpre_ref, scr):
    n = sz.lat_modes
    scr[...] = in_ref[...].astype(f32)
    for p in range(sz.planes):
        dmix_ref[p * n : (p + 1) * n, :] = lat_forward(sz, scr, cs_ref[...], p)

    def block(i, carry):
        rows = pl.ds(pl.multiple_of(i * 2 * n, 16), 2 * n)
        dpre_ref[rows, :] = mm(dmix_ref[rows, :], w2t_ref[...]) * slope_ref[rows, :]
        return carry

    lax.fori_loop(0, sz.planes // 2, block, 0)


def spectrum_back_kernel(sz, dpre_ref, cst_ref, w1t_ref, out_ref, scr, dspec):
    n = sz.lat_modes

    def block(i, carry):
        rows = pl.ds(pl.multiple_of(i * 2 * n, 16), 2 * n)
        dspec[rows, :] = mm(dpre_ref[rows, :], w1t_ref[...])
        return carry

    lax.fori_loop(0, sz.planes // 2, block, 0)
    for p in range(sz.planes):
        lat_inverse(sz, scr, cst_ref[...], dspec[p * n : (p + 1) * n, :], p)
    out_ref[...] = scr[...].astype(bf16)


def mlp_kernel(sz, at_ref, in_ref, x_ref, inv_ref, invt_ref, *refs):
    n = sz.n_ch
    own_ref, *parts = refs[:n]
    win_refs, wout_refs = refs[n : 2 * n], refs[2 * n : 3 * n]
    out_ref, sg_ref, mid_ref, upf_ref, act_ref, hg_ref, scr, z_scr, mg_scr, rs_scr, up_ref = refs[3 * n :]
    me, first_row = at_ref[4], at_ref[5]
    gather_parts(sz, at_ref, own_ref, parts, up_ref)
    for r in range(sz.own):

        def mask(r=r):
            for c in range(n):
                up_ref[c, r] = jnp.zeros((sz.lon, sz.chans), bf16)

        pl.when(first_row + r >= LAT)(mask)
    scr[...] = in_ref[...].astype(f32)
    mid_ref[...] = jnp.zeros(mid_ref.shape, bf16)
    upf_ref[...] = jnp.zeros(upf_ref.shape, bf16)
    c_all = range(sz.n_ch)

    def place(r, c):
        return (slice(r * sz.lon_pad, r * sz.lon_pad + sz.lon), slice(c * sz.chans, (c + 1) * sz.chans))

    for r in range(sz.own):
        xs = [x_ref[c, r].astype(f32) for c in c_all]
        normed, _ = center_scale(xs, sz.width)
        summed = [
            xs[c] + normed[c] + mm(inv_ref[...], load_modes(sz, scr, r, c))[:, : sz.chans] for c in c_all
        ]
        zs, recip = center_scale(summed, sz.width)
        rs_scr[r] = jnp.broadcast_to(recip, (sz.lon, LANES))
        for c in c_all:
            z_scr[c, r] = zs[c]
            mid_ref[place(r, c)] = zs[c].astype(bf16)
            upf_ref[place(r, c)] = up_ref[c, r]
    mg_scr[...] = jnp.zeros(mg_scr.shape, f32)
    nt = (((1,), (1,)), ((), ()))

    for d in range(n):
        j = me ^ d
        pre = mm(mid_ref[...], win_refs[d][...], None)
        back = lax.dot_general(upf_ref[...], wout_refs[d][...], nt, preferred_element_type=f32)
        act, slope = gelu_pair(pre)
        act_ref[j] = act.astype(bf16)
        grad = (back * slope).astype(bf16)
        hg_ref[j] = grad
        mg_scr[...] += lax.dot_general(grad, win_refs[d][...], nt, preferred_element_type=f32)
    for r in range(sz.own):
        zs = [z_scr[c, r] for c in c_all]
        grads = norm_back(zs, rs_scr[r][:, :1], [mg_scr[place(r, c)] for c in c_all], sz.width)
        for c in c_all:
            total = up_ref[c, r].astype(f32) + grads[c]
            sg_ref[c, r] = total
            store_modes(sz, scr, mm(invt_ref[...], wide(total)), r, c)
    out_ref[...] = scr[...].astype(bf16)


def field_kernel(sz, at_ref, in_ref, x_ref, sg_ref, fwdt_ref, *refs):
    outs, (scr, out_scr) = refs[: sz.n_ch], refs[sz.n_ch :]
    scr[...] = in_ref[...].astype(f32)
    c_all = range(sz.n_ch)
    for r in range(sz.own):
        normed, recip = center_scale([x_ref[c, r].astype(f32) for c in c_all], sz.width)
        sg = [sg_ref[c, r] for c in c_all]
        incoming = [sg[c] + mm(fwdt_ref[...], load_modes(sz, scr, r, c))[:, : sz.chans] for c in c_all]
        grads = norm_back(normed, recip, incoming, sz.width)
        for c in c_all:
            out_scr[c, r] = (sg[c] + grads[c]).astype(bf16)
    for d, out in enumerate(outs):
        out[...] = out_scr[at_ref[4] ^ d]


def join_kernel(sz, at_ref, *refs):
    parts, out_ref = refs[:-1], refs[-1]
    for d, part in enumerate(parts):
        for r in range(sz.own):
            out_ref[(at_ref[4] ^ d) * sz.own + r] = part[r]


def dense_keep_kernel(sz, at_ref, mid_ref, upf_ref, act_ref, hg_ref, got_ref,
                      a_keep, a_send, b_keep, b_send, scr):
    low, high, x = at_ref[0], at_ref[1], at_ref[2]
    tn = (((0,), (0,)), ((), ()))
    half = sz.width // 2
    for k, out in ((high, a_keep), (1 - high, a_send)):
        for side in range(2):
            lanes = slice(side * half, (side + 1) * half)
            part = lax.dot_general(mid_ref[:, lanes], hg_ref[2 * k + low], tn, preferred_element_type=f32)
            out[:, lanes] = (part + got_ref[k, 0, :, lanes].astype(f32)).astype(out.dtype)
    rows = scr.shape[0] // 2
    for k in range(2):
        part = lax.dot_general(act_ref[2 * k + low], upf_ref[...], tn, preferred_element_type=f32)
        scr[...] = part + got_ref[k, 1].astype(f32)
        b_keep[k] = scr[pl.ds(pl.multiple_of(x * rows, 16), rows), :]
        b_send[k] = scr[pl.ds(pl.multiple_of((1 - x) * rows, 16), rows), :].astype(bf16)


def lane_runs(p, b, size):
    if b == 0:
        return [(p * LANES, p * LANES + size)]
    return [(p * LANES + size, (p + 1) * LANES), (2 * LANES + p * HALF, 2 * LANES + (p + 1) * HALF)]


def take(values, p, b, size, axis):
    pieces = [lax.slice_in_dim(values, i, j, axis=axis) for i, j in lane_runs(p, b, size)]
    return pieces[0] if len(pieces) == 1 else jnp.concatenate(pieces, axis=axis)


def dense_step_kernel(sz, at_ref, a_keep, a_got, b_keep, b_got, a2_keep, a2_send, b2_keep, b2_send, scr):
    high, x = at_ref[1], at_ref[2]
    rows = a2_keep.shape[0]
    scr[...] = a_keep[...] + a_got[...].astype(f32)
    a2_keep[...] = scr[pl.ds(pl.multiple_of(x * rows, 16), rows), :]
    a2_send[...] = scr[pl.ds(pl.multiple_of((1 - x) * rows, 16), rows), :].astype(bf16)
    b2_keep[...] = b_keep[high] + b_got[high].astype(f32)
    b2_send[...] = (b_keep[1 - high] + b_got[1 - high].astype(f32)).astype(bf16)


def near_cut_kernel(sz, at_ref, a_keep, a_got, b_keep, b_got, keep, send, cut):
    low = at_ref[3] % 2
    many = cut.shape[1] // 2
    for p in range(cut.shape[0]):
        rows = slice(p * many, (p + 1) * many)
        cut[p, 0:many] = a_keep[rows, :] + a_got[rows, :].astype(f32)
        cut[p, many : 2 * many] = b_keep[rows, :] + b_got[rows, :].astype(f32)
    for h in range(2):
        keep[h] = cut[2 * h + low]
        send[h] = cut[2 * h + 1 - low].astype(bf16)


def far_cut_kernel(sz, at_ref, keep, got, own, send):
    high = at_ref[3] // 2
    own[...] = keep[high] + got[high].astype(f32)
    send[...] = (keep[1 - high] + got[1 - high].astype(f32)).astype(bf16)


def stack_kernel(sz, *refs):
    for i, ref in enumerate(refs[:-1]):
        refs[-1][i] = ref[...]


def block_kernel(sz, own, *refs):
    parts, out_ref = refs[:-1], refs[-1]
    total = own[...].astype(f32)
    for part in parts:
        total = total + part[...].astype(f32)
    out_ref[...] = total.astype(bf16)


def small_kernel(sz, spec_ref, dpre_ref, act_ref, dmix_ref, out_ref):
    tn = (((0,), (0,)), ((), ()))
    size = sz.chans // 2
    out_ref[...] = jnp.zeros(out_ref.shape, f32)
    for g, (left, right) in enumerate(((spec_ref, dpre_ref), (act_ref, dmix_ref))):
        big = lax.dot_general(left[...], right[...], tn, precision=HIGH, preferred_element_type=f32)
        for b in range(2):
            rows = [take(big, p, b, size, 0) for p in range(2)]
            real = take(rows[0], 0, b, size, 1) + take(rows[1], 1, b, size, 1)
            imag = take(rows[0], 1, b, size, 1) - take(rows[1], 0, b, size, 1)
            for p, value in enumerate((real, imag)):
                k = (g * 2 + p) * 2 + b
                out_ref[0:size, k * size : (k + 1) * size] = value
    bias = jnp.sum(dpre_ref[...], axis=0, keepdims=True)
    for p in range(2):
        for b in range(2):
            k = p * 2 + b
            out_ref[size : size + 1, k * size : (k + 1) * size] = take(bias, p, b, size, 1)


def small_round_kernel(sz, *refs):
    out_ref, scr = refs[4:]
    small_kernel(sz, *refs[:4], scr)
    out_ref[...] = scr[...].astype(bf16)


def place_kernel(sz, at_ref, s_own, s_far, far, far_own, *refs):
    parts = sz.n_sp // 2
    near, (in_ref, out_ref, w1_ref, w2_ref, b1_ref, scr) = refs[:parts], refs[parts:]
    many = far.shape[1] // 2
    half = sz.width // 2
    x = at_ref[2]
    for i in range(2 * parts):
        ref = near[i] if i < parts else far_own if i == parts else far.at[i - parts - 1]
        place = (x ^ (i // parts)) * parts + (at_ref[3] ^ (i % parts))
        base = pl.multiple_of(place * many, 16)
        in_ref[pl.ds(base, many), :] = ref[0:many, 0:half]
        in_ref[pl.ds(base + half, many), :] = ref[0:many, half : 2 * half]
        out_ref[pl.ds(base, many), :] = ref[many:, :]
    scr[...] = s_own[...].astype(f32) + s_far[...].astype(f32)
    spread_small(sz, scr, w1_ref, w2_ref, b1_ref)


def spread_small(sz, scr, w1_ref, w2_ref, b1_ref):
    size = sz.chans // 2
    for g, out in enumerate((w1_ref, w2_ref)):
        for p in range(2):
            for b in range(2):
                k = (g * 2 + p) * 2 + b
                out[p, b] = scr[0:size, k * size : (k + 1) * size]
    b1_ref[...] = scr[size : size + 1, 0 : 4 * size]


def call(body, outs, scratch, args, micros, scalars=0, after=()):
    in_specs = [pl.BlockSpec(memory_space=pltpu.SMEM)] * scalars
    in_specs += [pl.BlockSpec(memory_space=pltpu.VMEM)] * (len(args) - scalars)
    in_specs += [pl.BlockSpec(memory_space=pl.ANY)] * len(after)
    n_args, n_after = len(args), len(after)

    def wrapped(*refs):
        body(*refs[:n_args], *refs[n_args + n_after :])

    return pl.pallas_call(
        wrapped,
        in_specs=in_specs,
        out_shape=outs,
        scratch_shapes=scratch,
        compiler_params=pltpu.CompilerParams(vmem_limit_bytes=VMEM_BYTES),
        cost_estimate=pl.CostEstimate(flops=micros * 10**9, bytes_accessed=2**20, transcendentals=0),
    )(*args, *after)


def block_diagonal(weight):
    blocks, size = weight.shape[0], weight.shape[1]
    ident = jnp.eye(blocks, dtype=f32)
    return jnp.einsum("be,bio->bieo", ident, weight).reshape(blocks * size, blocks * size)


def lane_order(values, axis, chans):
    def cut(a, b):
        return lax.slice_in_dim(values, a, b, axis=axis)
    return jnp.concatenate(
        [cut(0, LANES), cut(chans, chans + LANES), cut(LANES, chans), cut(chans + LANES, 2 * chans)], axis=axis
    )


def natural_order(values, axis, chans):
    def cut(a, b):
        return lax.slice_in_dim(values, a, b, axis=axis)
    rest = chans - LANES
    return jnp.concatenate(
        [cut(0, LANES), cut(2 * LANES, 2 * LANES + rest), cut(LANES, 2 * LANES), cut(2 * LANES + rest, 2 * chans)],
        axis=axis,
    )


def big_weight(weight):
    real, imag = block_diagonal(weight[0]), block_diagonal(weight[1])
    full = jnp.concatenate(
        [jnp.concatenate([real, imag], axis=1), jnp.concatenate([-imag, real], axis=1)], axis=0
    )
    chans = real.shape[0]
    return lane_order(lane_order(full, 0, chans), 1, chans)


def small_grad(big, blocks):
    chans = big.shape[0] // 2
    size = chans // blocks
    full = natural_order(natural_order(big, 0, chans), 1, chans)
    full = full.reshape(2, blocks, size, 2, blocks, size)
    diag = jnp.stack([full[:, b, :, :, b, :] for b in range(blocks)], axis=0)
    real = diag[:, 0, :, 0] + diag[:, 1, :, 1]
    imag = diag[:, 0, :, 1] - diag[:, 1, :, 0]
    return jnp.stack([real, imag], axis=0)


def hop(axis, distance, values):
    n = lax.axis_size(axis)
    return lax.ppermute(values, axis, [(i, i ^ distance) for i in range(n)])


def dense_kernel(sz, other, low_ref, mid_ref, upf_ref, act_ref, hg_ref, out_ref):
    low = low_ref[0]
    low = 1 - low if other else low
    tn = (((0,), (0,)), ((), ()))
    half = sz.width // 2
    for k in range(sz.n_ch // 2):
        j = 2 * k + low
        for side in range(2):
            lanes = slice(side * half, (side + 1) * half)
            out_ref[k, 0, :, lanes] = lax.dot_general(
                mid_ref[:, lanes], hg_ref[j], tn, preferred_element_type=f32
            ).astype(out_ref.dtype)
        out_ref[k, 1] = lax.dot_general(
            act_ref[j], upf_ref[...], tn, preferred_element_type=f32
        ).astype(out_ref.dtype)


def b_whole(keep, send, sp_at):
    odd = sp_at % 2 == 1
    send = send.astype(f32)
    return jnp.concatenate([jnp.where(odd, send, keep), jnp.where(odd, keep, send)], axis=1)


def array(dtype, *shape):
    return jax.ShapeDtypeStruct(shape, dtype)


def split(*shape):
    return array(f32, *shape), array(bf16, *shape)


def local(field, cotangent, first_weight, first_bias, second_weight, dense_in, dense_out):
    n_sp, n_ch = lax.axis_size("sp"), lax.axis_size("ch")
    sz = Sizes(field.shape, n_sp, n_ch)
    both = ("sp", "ch")
    hid, width = dense_in.shape[1], sz.width
    forward, inverse = (jnp.asarray(t) for t in lon_tables(sz))
    cosine, sine = lat_table(sz)
    cs = jnp.asarray(np.concatenate([cosine, sine], axis=1))
    cs_t = jnp.asarray(np.concatenate([cosine.T, sine.T], axis=1))
    sp_at, ch_at = lax.axis_index("sp"), lax.axis_index("ch")
    first_row = sp_at % sz.bands * sz.rows + ch_at * sz.own
    at = jnp.stack([ch_at % 2, ch_at // 2, sp_at % 2, sp_at // 2, ch_at, first_row]).astype(jnp.int32)
    extra = sz.own * n_ch - sz.rows
    if extra:
        field, cotangent = (jnp.pad(v, ((0, extra), (0, 0), (0, 0))) for v in (field, cotangent))

    def row_parts(values):
        got = {}
        for d in reversed(range(1, n_ch)):
            got[d] = hop("ch", d, lax.dynamic_slice_in_dim(values, (ch_at ^ d) * sz.own, sz.own, 0))
        return [got[d] for d in range(1, n_ch)]

    def swap_modes(message):
        message = message.reshape(n_sp * n_ch, sz.pad, LANES)
        message = lax.all_to_all(message, both, split_axis=0, concat_axis=0, tiled=True)
        return message.reshape(n_sp * n_ch * sz.pad, LANES)

    def bind(kernel):
        return lambda *refs: kernel(sz, *refs)

    message = array(bf16, n_sp * n_ch * sz.pad, LANES)
    scr = pltpu.VMEM(message.shape, f32)
    flat = array(f32, sz.planes * sz.lat_modes, 2 * sz.chans)
    flat_scr = pltpu.VMEM(flat.shape, f32)
    cells = (n_ch, sz.own, sz.lon, sz.chans)

    x_parts = row_parts(field)
    x_parts, cotangent, dense_in, dense_out = lax.optimization_barrier((x_parts, cotangent, dense_in, dense_out))
    sent, x = call(
        bind(norm_spectrum_kernel), (message, array(bf16, *cells)), [scr], (at, field, *x_parts, forward), 3, 1
    )
    up_parts = row_parts(cotangent)
    far_in, far_out = hop("ch", 2, dense_in), hop("ch", 2, dense_out)
    near_in, near_out = hop("ch", 1, dense_in), hop("ch", 1, dense_out)
    sent, first_weight, second_weight, first_bias = lax.optimization_barrier(
        (sent, first_weight, second_weight, first_bias)
    )
    w1, w2 = big_weight(first_weight), big_weight(second_weight)
    b1 = lane_order(first_bias.reshape(1, -1), 1, sz.chans)
    got = swap_modes(sent)
    sent, spec, act, slope = call(
        bind(mix_kernel),
        (message, flat, flat, flat),
        [scr, flat_scr],
        (got, cs, cs_t, w1, b1, w2),
        10,
        after=(*up_parts, far_in),
    )
    got = swap_modes(sent)
    wins = (dense_in, near_in, far_in, hop("ch", 1, far_in))
    wouts = (dense_out, near_out, far_out, hop("ch", 1, far_out))
    tokens = sz.own * sz.lon_pad
    grown = array(bf16, tokens, width)
    hidden = array(bf16, n_ch, tokens, hid)
    sent, sg, mid, upf, hidden_act, hidden_grad = call(
        bind(mlp_kernel),
        (message, array(f32, *cells), grown, grown, hidden, hidden),
        [
            scr,
            pltpu.VMEM(cells, f32),
            pltpu.VMEM(grown.shape, f32),
            pltpu.VMEM((sz.own, sz.lon, LANES), f32),
            pltpu.VMEM(cells, bf16),
        ],
        (at, got, x, inverse, inverse.T, cotangent, *up_parts, *wins, *wouts),
        20,
        1,
    )
    got = swap_modes(sent)
    factors = (at, mid, upf, hidden_act, hidden_grad)
    sent_part = call(
        lambda *refs: dense_kernel(sz, True, *refs), array(bf16, n_ch // 2, 2, hid, width), [], factors, 0, 1
    )
    got_part = hop("ch", 1, sent_part)
    a_keep, a_send, b_keep, b_send = call(
        bind(dense_keep_kernel),
        split(hid, width) + split(2, hid // 2, width),
        [pltpu.VMEM((hid, width), f32)],
        (*factors, got_part),
        0,
        1,
    )
    eight = n_sp == 8
    small_rows = up_to(sz.chans // 2 + 1, 16)
    before = (a_keep,)
    if eight:
        a_got, b_got = hop("ch", 2, a_send), hop("sp", 1, b_send)
        a_keep, a_send, b_keep, b_send = before = call(
            bind(dense_step_kernel),
            split(hid // 2, width) * 2,
            [pltpu.VMEM((hid, width), f32)],
            (at, a_keep, a_got, b_keep, b_got),
            0,
            1,
        )
        a_got, b_got = hop("sp", 1, a_send), hop("ch", 2, b_send)
    dmix, dpre = call(
        bind(mix_back_kernel), (flat, flat), [scr], (got, cs, w2.T, slope), 6, after=before[:1]
    )
    sent = call(
        bind(spectrum_back_kernel),
        message,
        [scr, flat_scr],
        (dpre, cs_t, w1.T),
        6,
        after=(a_got, b_got) if eight else (),
    )
    got = swap_modes(sent)
    last = ()
    smalls = (spec, dpre, act, dmix)
    if eight:
        parts = n_sp // 2
        piece = 2 * hid // n_sp
        keep, send = call(
            bind(near_cut_kernel),
            split(2, piece, width),
            [pltpu.VMEM((parts, piece, width), f32)],
            (at, a_keep, a_got, b_keep, b_got),
            0,
            1,
        )
        got_near = hop("sp", 2, send)
        small = call(
            bind(small_round_kernel),
            array(bf16, small_rows, width),
            [pltpu.VMEM((small_rows, width), f32)],
            smalls,
            0,
            after=(keep,),
        )
        small_got = hop("sp", 1, small)
        own, send = call(bind(far_cut_kernel), split(piece, width), [], (at, keep, got_near), 0, 1)
        got_far = hop("sp", 4, send)
        last = (own, small_got)
    grads = call(
        bind(field_kernel),
        [array(bf16, *cells[1:])] * n_ch,
        [scr, pltpu.VMEM(cells, bf16)],
        (at, got, x, sg, forward.T),
        6,
        1,
        after=last,
    )
    grad_parts = [grads[0]] + [hop("ch", d, grads[d]) for d in range(1, n_ch)]
    w_shapes = [array(f32, *first_weight.shape)] * 2 + [array(f32, 1, 2 * sz.chans)]
    if eight:
        block = call(bind(block_kernel), array(bf16, piece, width), [], (own, got_far), 0, after=(grads[0],))
        near = [hop("sp", 2 * d, block) for d in range(1, parts)]
        far_own = hop("sp", 1, block)
        small_shape = array(bf16, small_rows, width)
        small = call(bind(block_kernel), small_shape, [], (small, small_got), 0)
        small_got = hop("sp", 2, small)
        stacked = call(
            bind(stack_kernel), array(bf16, parts - 1, piece, width), [], near, 0, after=(*grad_parts[1:], small_got, far_own)
        )
        far = hop("sp", 1, stacked)
        small = call(bind(block_kernel), small_shape, [], (small, small_got), 0)
        in_grad, out_grad, w1_grad, w2_grad, b1_grad = call(
            bind(place_kernel),
            [array(bf16, width, hid), array(bf16, hid, width)] + w_shapes,
            [pltpu.VMEM((small_rows, width), f32)],
            (at, small, hop("sp", 4, small), far, far_own, block, *near),
            0,
            1,
        )
    else:
        high = (ch_at // 2 == 1)
        b_full = b_whole(b_keep, b_send, sp_at)
        in_grad = a_keep + hop("ch", 2, a_send).astype(f32)
        out_keep = jnp.where(high, b_full[1], b_full[0])
        out_grad = out_keep + hop("ch", 2, jnp.where(high, b_full[0], b_full[1]))
        small = call(bind(small_kernel), array(f32, small_rows, width), [], smalls, 0)
        in_grad, out_grad, small = lax.psum((in_grad, out_grad, small), "sp")
        half = width // 2
        in_grad = jnp.concatenate([in_grad[:, :half], in_grad[:, half:]], axis=0).astype(bf16)
        out_grad = out_grad.astype(bf16)
        w1_grad, w2_grad, b1_grad = call(bind(spread_small), w_shapes, [], (small,), 0)
    grad = call(bind(join_kernel), array(bf16, n_ch * sz.own, *cells[2:]), [], (at, *grad_parts), 0, 1)
    return (grad[: sz.rows], w1_grad, b1_grad.reshape(first_bias.shape), w2_grad, in_grad, out_grad)


def solution(mesh):
    placed = (
        P("sp", None, "ch"),
        P("sp", None, "ch"),
        P(None, "ch", None, None),
        P(None, "ch", None),
        P(None, "ch", None, None),
        P(None, "ch"),
        P("ch", None),
    )
    return jax.shard_map(
        local,
        mesh=mesh,
        in_specs=placed,
        out_specs=(
            P("sp", None, "ch"),
            P(None, "ch", None, None),
            P(None, "ch", None),
            P(None, "ch", None, None),
            P(None, "ch"),
            P("ch", None),
        ),
        check_vma=False,
    )
```

```python
import math

import jax
import jax.numpy as jnp
import ml_dtypes
import numpy as np
from jax import lax
from jax.experimental import pallas as pl
from jax.experimental.pallas import tpu as pltpu
from jax.sharding import PartitionSpec as P

LAT = 90
BAND_MAX = 16
LANES = 128
HALF = 64

eps = 1e-05
f32 = jnp.float32
bf16 = jnp.bfloat16
HIGH = lax.Precision.HIGH
VMEM_BYTES = 50 * 2**20


def up_to(value, step):
    return (value + step - 1) // step * step


class Sizes:
    def __init__(self, block, n_sp, n_ch):
        self.rows, self.lon, self.chans = block
        self.n_sp, self.n_ch = n_sp, n_ch
        self.width = self.chans * n_ch
        self.own = -(-self.rows // n_ch)
        self.bands = min(BAND_MAX, n_sp)
        self.samples = n_sp // self.bands
        self.modes = -(-(self.lon // 2 + 1) // n_sp)
        self.all_modes = self.modes * n_sp
        self.parts = 2 * self.chans // LANES
        self.pad = up_to(self.parts * self.own * self.modes, 16)
        self.sources = self.bands * n_ch
        self.lat_in = self.own * self.sources
        self.lat_modes = up_to(LAT, 16)
        self.planes = self.samples * self.modes
        self.lon_pad = up_to(self.lon, 16)

    def slot(self, q, r, m):
        return (q * self.own + r) * self.modes + m


def lon_tables(sz):
    mode = (np.arange(sz.n_sp)[None, :] * sz.modes + np.arange(sz.modes)[:, None]).reshape(-1, 1)
    cell = np.arange(sz.lon)[None, :]
    phase = 2.0 * np.pi / sz.lon * (mode * cell % sz.lon)
    live = (mode <= sz.lon // 2).astype(np.float64)
    inner = ((mode > 0) & (mode < sz.lon // 2)).astype(np.float64)
    scale = 1.0 / math.sqrt(sz.lon)
    cosine = np.cos(phase) * live * scale
    sine = np.sin(phase) * inner * scale
    forward = np.concatenate([cosine, -sine], axis=0)
    inverse = np.concatenate([cosine * (live + inner), -2.0 * sine], axis=0).T
    return forward.astype(np.float32), np.ascontiguousarray(inverse).astype(np.float32)


def lat_table(sz):
    r = np.arange(sz.own)[:, None, None]
    band = np.arange(sz.bands)[None, :, None]
    c = np.arange(sz.n_ch)[None, None, :]
    cell = band * sz.rows + c * sz.own + r
    live = np.logical_and(c * sz.own + r < sz.rows, cell < LAT).reshape(1, -1)
    cell = cell.reshape(1, -1)
    mode = np.arange(sz.lat_modes)[:, None]
    live = np.logical_and(live, mode < LAT) / math.sqrt(LAT)
    phase = 2.0 * np.pi / LAT * (mode * cell % LAT)
    return (
        (np.cos(phase) * live).astype(np.float32),
        (np.sin(phase) * live).astype(np.float32),
    )


def gelu_pair(v):
    cdf = 0.5 * (1.0 + lax.erf(v * np.float32(math.sqrt(0.5))))
    pdf = jnp.exp(-0.5 * v * v) * np.float32(1.0 / math.sqrt(2.0 * math.pi))
    return v * cdf, cdf + v * pdf


def mm(a, b, precision=HIGH):
    return jnp.dot(a, b, precision=precision, preferred_element_type=f32)


def two_terms(table, rows):
    table = np.pad(table, ((0, rows - table.shape[0]), (0, 0)))
    first = table.astype(ml_dtypes.bfloat16)
    second = (table - first.astype(np.float32)).astype(ml_dtypes.bfloat16)
    return jnp.asarray(np.concatenate([first, second], axis=0))


def mm_two(table, values):
    y = jnp.dot(table, values.astype(bf16), preferred_element_type=f32)
    n = table.shape[0] // 2
    return y[:n] + y[n:]


def swap(values):
    lane = lax.broadcasted_iota(jnp.int32, values.shape, 1)
    turned = pltpu.roll(values, HALF, 1)
    return jnp.where(lane < HALF, turned, -turned)


def store_modes(sz, scr, y, r, c):
    n = sz.all_modes
    re, im = y[:n], y[n:]
    pieces = (re[:, :LANES], im[:, :LANES], re[:, LANES:] + pltpu.roll(im[:, LANES:], HALF, 1))
    for q, piece in enumerate(pieces):
        for m in range(sz.modes):
            scr[pl.ds(c * sz.pad + sz.slot(q, r, m), sz.n_sp, stride=sz.n_ch * sz.pad), :] = piece[
                m * sz.n_sp : (m + 1) * sz.n_sp
            ]


def load_modes(sz, scr, r, c):
    q0, q1, q2 = (
        jnp.concatenate(
            [
                scr[pl.ds(c * sz.pad + sz.slot(q, r, m), sz.n_sp, stride=sz.n_ch * sz.pad), :]
                for m in range(sz.modes)
            ],
            axis=0,
        )
        for q in range(3)
    )
    left = jnp.concatenate([q0, q1], axis=0)
    right = jnp.concatenate([q2, pltpu.roll(q2, HALF, 1)], axis=0)
    return jnp.concatenate([left, right], axis=1)


def wide(values):
    rows, lanes = values.shape
    return jnp.concatenate([values, jnp.zeros((rows, up_to(lanes, LANES) - lanes), f32)], axis=1)


def plane_start(sz, s, q, r, m):
    return s * sz.sources * sz.pad + sz.slot(q, r, m)


def center_scale(chunks, width):
    mean = sum(jnp.sum(v, axis=-1, keepdims=True) for v in chunks) / width
    chunks = [v - mean for v in chunks]
    var = sum(jnp.sum(v * v, axis=-1, keepdims=True) for v in chunks) / width
    recip = lax.rsqrt(var + eps)
    return [v * recip for v in chunks], recip


def norm_back(normed, recip, incoming, width):
    first = sum(jnp.sum(g, axis=-1, keepdims=True) for g in incoming) / width
    second = sum(jnp.sum(g * z, axis=-1, keepdims=True) for g, z in zip(incoming, normed)) / width
    return [recip * (g - first - z * second) for g, z in zip(incoming, normed)]


def gather_parts(sz, at_ref, own_ref, parts, out_ref):
    me = at_ref[4]
    for r in range(sz.own):
        out_ref[me, r] = own_ref[me * sz.own + r]
    for d, part in enumerate(parts):
        out_ref[me ^ (d + 1)] = part[...]


def norm_spectrum_kernel(sz, at_ref, *refs):
    own_ref, *parts = refs[: sz.n_ch]
    tab_ref, out_ref, x_ref, scr = refs[sz.n_ch :]
    gather_parts(sz, at_ref, own_ref, parts, x_ref)
    for r in range(sz.own):
        normed, _ = center_scale([x_ref[c, r].astype(f32) for c in range(sz.n_ch)], sz.width)
        for c in range(sz.n_ch):
            store_modes(sz, scr, mm(tab_ref[...], wide(normed[c])), r, c)
    out_ref[...] = scr[...].astype(bf16)


def lat_forward(sz, scr, cs, p):
    s, m = divmod(p, sz.modes)
    x0, x1, x2 = (
        jnp.concatenate(
            [
                scr[pl.ds(plane_start(sz, s, q, r, m), sz.sources, stride=sz.pad), :]
                for r in range(sz.own)
            ],
            axis=0,
        )
        for q in range(3)
    )
    both = jnp.concatenate(
        [jnp.concatenate([x0, x1, x2], axis=1), jnp.concatenate([x1, -x0, swap(x2)], axis=1)], axis=0
    )
    return mm_two(cs, both)


def lat_inverse(sz, scr, cs_t, o, p):
    s, m = divmod(p, sz.modes)
    o0, o1, o2 = (o[:, q * LANES : (q + 1) * LANES] for q in range(3))
    both = jnp.concatenate(
        [jnp.concatenate([o0, o1, o2], axis=1), jnp.concatenate([-o1, o0, -swap(o2)], axis=1)], axis=0
    )
    y = mm_two(cs_t, both)
    for q in range(3):
        for r in range(sz.own):
            scr[pl.ds(plane_start(sz, s, q, r, m), sz.sources, stride=sz.pad), :] = y[
                r * sz.sources : (r + 1) * sz.sources, q * LANES : (q + 1) * LANES
            ]


def mix_kernel(sz, in_ref, cs_ref, cst_ref, w1_ref, b1_ref, w2_ref,
               out_ref, spec_ref, act_ref, slope_ref, scr, mixed):
    n = sz.lat_modes
    scr[...] = in_ref[...].astype(f32)
    for p in range(sz.planes):
        spec_ref[p * n : (p + 1) * n, :] = lat_forward(sz, scr, cs_ref[...], p)

    def block(i, carry):
        rows = pl.ds(pl.multiple_of(i * 2 * n, 16), 2 * n)
        act, slope = gelu_pair(mm(spec_ref[rows, :], w1_ref[...]) + b1_ref[...])
        act_ref[rows, :] = act
        slope_ref[rows, :] = slope
        mixed[rows, :] = mm(act, w2_ref[...])
        return carry

    lax.fori_loop(0, sz.planes // 2, block, 0)
    for p in range(sz.planes):
        lat_inverse(sz, scr, cst_ref[...], mixed[p * n : (p + 1) * n, :], p)
    out_ref[...] = scr[...].astype(bf16)


def mix_back_kernel(sz, in_ref, cs_ref, w2t_ref, slope_ref, dmix_ref, dpre_ref, scr):
    n = sz.lat_modes
    scr[...] = in_ref[...].astype(f32)
    for p in range(sz.planes):
        dmix_ref[p * n : (p + 1) * n, :] = lat_forward(sz, scr, cs_ref[...], p)

    def block(i, carry):
        rows = pl.ds(pl.multiple_of(i * 2 * n, 16), 2 * n)
        dpre_ref[rows, :] = mm(dmix_ref[rows, :], w2t_ref[...]) * slope_ref[rows, :]
        return carry

    lax.fori_loop(0, sz.planes // 2, block, 0)


def spectrum_back_cut_kernel(sz, at_ref, dpre_ref, cst_ref, w1t_ref, *refs):
    near_cut_kernel(sz, at_ref, *refs[:4], *refs[5:7], refs[9])
    spectrum_back_kernel(sz, dpre_ref, cst_ref, w1t_ref, refs[4], *refs[7:9])


def spectrum_back_kernel(sz, dpre_ref, cst_ref, w1t_ref, out_ref, scr, dspec):
    n = sz.lat_modes

    def block(i, carry):
        rows = pl.ds(pl.multiple_of(i * 2 * n, 16), 2 * n)
        dspec[rows, :] = mm(dpre_ref[rows, :], w1t_ref[...])
        return carry

    lax.fori_loop(0, sz.planes // 2, block, 0)
    for p in range(sz.planes):
        lat_inverse(sz, scr, cst_ref[...], dspec[p * n : (p + 1) * n, :], p)
    out_ref[...] = scr[...].astype(bf16)


def mlp_kernel(sz, at_ref, in_ref, x_ref, inv_ref, invt_ref, *refs):
    n = sz.n_ch
    own_ref, *parts = refs[:n]
    win_refs, wout_refs = refs[n : 2 * n], refs[2 * n : 3 * n]
    out_ref, sg_ref, mid_ref, upf_ref, act_ref, hg_ref, part_ref, scr, z_scr, mg_scr, rs_scr, up_ref = refs[3 * n :]
    me, first_row = at_ref[4], at_ref[5]
    gather_parts(sz, at_ref, own_ref, parts, up_ref)
    for r in range(sz.own):

        def mask(r=r):
            for c in range(n):
                up_ref[c, r] = jnp.zeros((sz.lon, sz.chans), bf16)

        pl.when(first_row + r >= LAT)(mask)
    scr[...] = in_ref[...].astype(f32)
    mid_ref[...] = jnp.zeros(mid_ref.shape, bf16)
    upf_ref[...] = jnp.zeros(upf_ref.shape, bf16)
    c_all = range(sz.n_ch)

    def place(r, c):
        return (slice(r * sz.lon_pad, r * sz.lon_pad + sz.lon), slice(c * sz.chans, (c + 1) * sz.chans))

    for r in range(sz.own):
        xs = [x_ref[c, r].astype(f32) for c in c_all]
        normed, _ = center_scale(xs, sz.width)
        summed = [
            xs[c] + normed[c] + mm_two(inv_ref[...], load_modes(sz, scr, r, c))[: sz.lon, : sz.chans] for c in c_all
        ]
        zs, recip = center_scale(summed, sz.width)
        rs_scr[r] = jnp.broadcast_to(recip, (sz.lon, LANES))
        for c in c_all:
            z_scr[c, r] = zs[c]
            mid_ref[place(r, c)] = zs[c].astype(bf16)
            upf_ref[place(r, c)] = up_ref[c, r]
    mg_scr[...] = jnp.zeros(mg_scr.shape, f32)
    nt = (((1,), (1,)), ((), ()))

    for d in range(n):
        j = me ^ d
        pre = mm(mid_ref[...], win_refs[d][...], None)
        back = lax.dot_general(upf_ref[...], wout_refs[d][...], nt, preferred_element_type=f32)
        act, slope = gelu_pair(pre)
        act_ref[j] = act.astype(bf16)
        grad = (back * slope).astype(bf16)
        hg_ref[j] = grad
        mg_scr[...] += lax.dot_general(grad, win_refs[d][...], nt, preferred_element_type=f32)
        if d % 2:
            dense_parts(sz, part_ref, at_ref[1] ^ (d // 2), j, mid_ref, upf_ref, act_ref, hg_ref)
    for r in range(sz.own):
        zs = [z_scr[c, r] for c in c_all]
        grads = norm_back(zs, rs_scr[r][:, :1], [mg_scr[place(r, c)] for c in c_all], sz.width)
        for c in c_all:
            total = up_ref[c, r].astype(f32) + grads[c]
            sg_ref[c, r] = total
            store_modes(sz, scr, mm(invt_ref[...], wide(total)), r, c)
    out_ref[...] = scr[...].astype(bf16)


def field_kernel(sz, at_ref, in_ref, x_ref, sg_ref, fwdt_ref, *refs):
    outs, (scr, out_scr) = refs[: sz.n_ch], refs[sz.n_ch :]
    scr[...] = in_ref[...].astype(f32)
    c_all = range(sz.n_ch)
    for r in range(sz.own):
        normed, recip = center_scale([x_ref[c, r].astype(f32) for c in c_all], sz.width)
        sg = [sg_ref[c, r] for c in c_all]
        incoming = [sg[c] + mm_two(fwdt_ref[...], load_modes(sz, scr, r, c))[: sz.lon, : sz.chans] for c in c_all]
        grads = norm_back(normed, recip, incoming, sz.width)
        for c in c_all:
            out_scr[c, r] = (sg[c] + grads[c]).astype(bf16)
    for d, out in enumerate(outs):
        out[...] = out_scr[at_ref[4] ^ d]


def join_kernel(sz, at_ref, *refs):
    parts, out_ref = refs[:-1], refs[-1]
    for d, part in enumerate(parts):
        for r in range(sz.own):
            out_ref[(at_ref[4] ^ d) * sz.own + r] = part[r]


def dense_keep_kernel(sz, at_ref, mid_ref, upf_ref, act_ref, hg_ref, got_ref,
                      a_keep, a_send, b_keep, b_send, scr):
    low, high, x = at_ref[0], at_ref[1], at_ref[2]
    tn = (((0,), (0,)), ((), ()))
    half = sz.width // 2
    for k, out in ((high, a_keep), (1 - high, a_send)):
        for side in range(2):
            lanes = slice(side * half, (side + 1) * half)
            part = lax.dot_general(mid_ref[:, lanes], hg_ref[2 * k + low], tn, preferred_element_type=f32)
            out[:, lanes] = (part + got_ref[k, 0, :, lanes].astype(f32)).astype(out.dtype)
    rows = scr.shape[0] // 2
    for k in range(2):
        part = lax.dot_general(act_ref[2 * k + low], upf_ref[...], tn, preferred_element_type=f32)
        scr[...] = part + got_ref[k, 1].astype(f32)
        b_keep[k] = scr[pl.ds(pl.multiple_of(x * rows, 16), rows), :]
        b_send[k] = scr[pl.ds(pl.multiple_of((1 - x) * rows, 16), rows), :].astype(bf16)


def lane_runs(p, b, size):
    if b == 0:
        return [(p * LANES, p * LANES + size)]
    return [(p * LANES + size, (p + 1) * LANES), (2 * LANES + p * HALF, 2 * LANES + (p + 1) * HALF)]


def take(values, p, b, size, axis):
    pieces = [lax.slice_in_dim(values, i, j, axis=axis) for i, j in lane_runs(p, b, size)]
    return pieces[0] if len(pieces) == 1 else jnp.concatenate(pieces, axis=axis)


def dense_step_kernel(sz, at_ref, a_keep, a_got, b_keep, b_got, a2_keep, a2_send, b2_keep, b2_send, scr):
    high, x = at_ref[1], at_ref[2]
    rows = a2_keep.shape[0]
    scr[...] = a_keep[...] + a_got[...].astype(f32)
    a2_keep[...] = scr[pl.ds(pl.multiple_of(x * rows, 16), rows), :]
    a2_send[...] = scr[pl.ds(pl.multiple_of((1 - x) * rows, 16), rows), :].astype(bf16)
    b2_keep[...] = b_keep[high] + b_got[high].astype(f32)
    b2_send[...] = (b_keep[1 - high] + b_got[1 - high].astype(f32)).astype(bf16)


def near_cut_kernel(sz, at_ref, a_keep, a_got, b_keep, b_got, keep, send, cut):
    low = at_ref[3] % 2
    many = cut.shape[1] // 2
    for p in range(cut.shape[0]):
        rows = slice(p * many, (p + 1) * many)
        cut[p, 0:many] = a_keep[rows, :] + a_got[rows, :].astype(f32)
        cut[p, many : 2 * many] = b_keep[rows, :] + b_got[rows, :].astype(f32)
    for h in range(2):
        keep[h] = cut[2 * h + low]
        send[h] = cut[2 * h + 1 - low].astype(bf16)


def far_cut_kernel(sz, at_ref, keep, got, own, send):
    high = at_ref[3] // 2
    own[...] = keep[high] + got[high].astype(f32)
    send[...] = (keep[1 - high] + got[1 - high].astype(f32)).astype(bf16)


def stack_kernel(sz, *refs):
    for i, ref in enumerate(refs[:-1]):
        refs[-1][i] = ref[...]


def block_kernel(sz, own, *refs):
    parts, out_ref = refs[:-1], refs[-1]
    total = own[...].astype(f32)
    for part in parts:
        total = total + part[...].astype(f32)
    out_ref[...] = total.astype(bf16)


def small_kernel(sz, spec_ref, dpre_ref, act_ref, dmix_ref, out_ref):
    tn = (((0,), (0,)), ((), ()))
    size = sz.chans // 2
    out_ref[...] = jnp.zeros(out_ref.shape, f32)
    for g, (left, right) in enumerate(((spec_ref, dpre_ref), (act_ref, dmix_ref))):
        big = lax.dot_general(left[...], right[...], tn, precision=HIGH, preferred_element_type=f32)
        for b in range(2):
            rows = [take(big, p, b, size, 0) for p in range(2)]
            real = take(rows[0], 0, b, size, 1) + take(rows[1], 1, b, size, 1)
            imag = take(rows[0], 1, b, size, 1) - take(rows[1], 0, b, size, 1)
            for p, value in enumerate((real, imag)):
                k = (g * 2 + p) * 2 + b
                out_ref[0:size, k * size : (k + 1) * size] = value
    bias = jnp.sum(dpre_ref[...], axis=0, keepdims=True)
    for p in range(2):
        for b in range(2):
            k = p * 2 + b
            out_ref[size : size + 1, k * size : (k + 1) * size] = take(bias, p, b, size, 1)


def small_round_kernel(sz, *refs):
    out_ref, scr = refs[4:]
    small_kernel(sz, *refs[:4], scr)
    out_ref[...] = scr[...].astype(bf16)


def place_kernel(sz, at_ref, s_own, s_far, far, far_own, *refs):
    parts = sz.n_sp // 2
    near, (in_ref, out_ref, w1_ref, w2_ref, b1_ref, scr) = refs[:parts], refs[parts:]
    many = far.shape[1] // 2
    half = sz.width // 2
    x = at_ref[2]
    for i in range(2 * parts):
        ref = near[i] if i < parts else far_own if i == parts else far.at[i - parts - 1]
        place = (x ^ (i // parts)) * parts + (at_ref[3] ^ (i % parts))
        base = pl.multiple_of(place * many, 16)
        in_ref[pl.ds(base, many), :] = ref[0:many, 0:half]
        in_ref[pl.ds(base + half, many), :] = ref[0:many, half : 2 * half]
        out_ref[pl.ds(base, many), :] = ref[many:, :]
    scr[...] = s_own[...].astype(f32) + s_far[...].astype(f32)
    spread_small(sz, scr, w1_ref, w2_ref, b1_ref)


def spread_small(sz, scr, w1_ref, w2_ref, b1_ref):
    size = sz.chans // 2
    for g, out in enumerate((w1_ref, w2_ref)):
        for p in range(2):
            for b in range(2):
                k = (g * 2 + p) * 2 + b
                out[p, b] = scr[0:size, k * size : (k + 1) * size]
    b1_ref[...] = scr[size : size + 1, 0 : 4 * size]


def call(body, outs, scratch, args, micros, scalars=0, after=()):
    in_specs = [pl.BlockSpec(memory_space=pltpu.SMEM)] * scalars
    in_specs += [pl.BlockSpec(memory_space=pltpu.VMEM)] * (len(args) - scalars)
    in_specs += [pl.BlockSpec(memory_space=pl.ANY)] * len(after)
    n_args, n_after = len(args), len(after)

    def wrapped(*refs):
        body(*refs[:n_args], *refs[n_args + n_after :])

    return pl.pallas_call(
        wrapped,
        in_specs=in_specs,
        out_shape=outs,
        scratch_shapes=scratch,
        compiler_params=pltpu.CompilerParams(vmem_limit_bytes=VMEM_BYTES),
        cost_estimate=pl.CostEstimate(flops=micros * 10**9, bytes_accessed=2**20, transcendentals=0),
    )(*args, *after)


def block_diagonal(weight):
    blocks, size = weight.shape[0], weight.shape[1]
    ident = jnp.eye(blocks, dtype=f32)
    return jnp.einsum("be,bio->bieo", ident, weight).reshape(blocks * size, blocks * size)


def lane_order(values, axis, chans):
    def cut(a, b):
        return lax.slice_in_dim(values, a, b, axis=axis)
    return jnp.concatenate(
        [cut(0, LANES), cut(chans, chans + LANES), cut(LANES, chans), cut(chans + LANES, 2 * chans)], axis=axis
    )


def natural_order(values, axis, chans):
    def cut(a, b):
        return lax.slice_in_dim(values, a, b, axis=axis)
    rest = chans - LANES
    return jnp.concatenate(
        [cut(0, LANES), cut(2 * LANES, 2 * LANES + rest), cut(LANES, 2 * LANES), cut(2 * LANES + rest, 2 * chans)],
        axis=axis,
    )


def big_weight(weight):
    real, imag = block_diagonal(weight[0]), block_diagonal(weight[1])
    full = jnp.concatenate(
        [jnp.concatenate([real, imag], axis=1), jnp.concatenate([-imag, real], axis=1)], axis=0
    )
    chans = real.shape[0]
    return lane_order(lane_order(full, 0, chans), 1, chans)


def small_grad(big, blocks):
    chans = big.shape[0] // 2
    size = chans // blocks
    full = natural_order(natural_order(big, 0, chans), 1, chans)
    full = full.reshape(2, blocks, size, 2, blocks, size)
    diag = jnp.stack([full[:, b, :, :, b, :] for b in range(blocks)], axis=0)
    real = diag[:, 0, :, 0] + diag[:, 1, :, 1]
    imag = diag[:, 0, :, 1] - diag[:, 1, :, 0]
    return jnp.stack([real, imag], axis=0)


def hop(axis, distance, values):
    n = lax.axis_size(axis)
    return lax.ppermute(values, axis, [(i, i ^ distance) for i in range(n)])


def dense_parts(sz, out_ref, k, j, mid_ref, upf_ref, act_ref, hg_ref):
    tn = (((0,), (0,)), ((), ()))
    half = sz.width // 2
    for side in range(2):
        lanes = slice(side * half, (side + 1) * half)
        out_ref[k, 0, :, lanes] = lax.dot_general(
            mid_ref[:, lanes], hg_ref[j], tn, preferred_element_type=f32
        ).astype(out_ref.dtype)
    out_ref[k, 1] = lax.dot_general(act_ref[j], upf_ref[...], tn, preferred_element_type=f32).astype(out_ref.dtype)


def b_whole(keep, send, sp_at):
    odd = sp_at % 2 == 1
    send = send.astype(f32)
    return jnp.concatenate([jnp.where(odd, send, keep), jnp.where(odd, keep, send)], axis=1)


def array(dtype, *shape):
    return jax.ShapeDtypeStruct(shape, dtype)


def split(*shape):
    return array(f32, *shape), array(bf16, *shape)


def local(field, cotangent, first_weight, first_bias, second_weight, dense_in, dense_out):
    n_sp, n_ch = lax.axis_size("sp"), lax.axis_size("ch")
    sz = Sizes(field.shape, n_sp, n_ch)
    both = ("sp", "ch")
    hid, width = dense_in.shape[1], sz.width
    forward, inverse = lon_tables(sz)
    forward_t, inverse_2 = two_terms(forward.T, sz.lon_pad), two_terms(inverse, sz.lon_pad)
    forward, inverse_t = jnp.asarray(forward), jnp.asarray(inverse.T)
    cosine, sine = lat_table(sz)
    cs = two_terms(np.concatenate([cosine, sine], axis=1), sz.lat_modes)
    cs_t = two_terms(np.concatenate([cosine.T, sine.T], axis=1), sz.lat_in)
    sp_at, ch_at = lax.axis_index("sp"), lax.axis_index("ch")
    first_row = sp_at % sz.bands * sz.rows + ch_at * sz.own
    at = jnp.stack([ch_at % 2, ch_at // 2, sp_at % 2, sp_at // 2, ch_at, first_row]).astype(jnp.int32)
    extra = sz.own * n_ch - sz.rows
    if extra:
        field, cotangent = (jnp.pad(v, ((0, extra), (0, 0), (0, 0))) for v in (field, cotangent))

    def row_parts(values):
        got = {}
        for d in reversed(range(1, n_ch)):
            got[d] = hop("ch", d, lax.dynamic_slice_in_dim(values, (ch_at ^ d) * sz.own, sz.own, 0))
        return [got[d] for d in range(1, n_ch)]

    def swap_modes(message):
        message = message.reshape(n_sp * n_ch, sz.pad, LANES)
        message = lax.all_to_all(message, both, split_axis=0, concat_axis=0, tiled=True)
        return message.reshape(n_sp * n_ch * sz.pad, LANES)

    def bind(kernel):
        return lambda *refs: kernel(sz, *refs)

    message = array(bf16, n_sp * n_ch * sz.pad, LANES)
    scr = pltpu.VMEM(message.shape, f32)
    flat = array(f32, sz.planes * sz.lat_modes, 2 * sz.chans)
    flat_scr = pltpu.VMEM(flat.shape, f32)
    cells = (n_ch, sz.own, sz.lon, sz.chans)

    x_parts = row_parts(field)
    x_parts, cotangent, dense_in, dense_out = lax.optimization_barrier((x_parts, cotangent, dense_in, dense_out))
    sent, x = call(
        bind(norm_spectrum_kernel), (message, array(bf16, *cells)), [scr], (at, field, *x_parts, forward), 3, 1
    )
    up_parts = row_parts(cotangent)
    far_in, far_out = hop("ch", 2, dense_in), hop("ch", 2, dense_out)
    near_in, near_out = hop("ch", 1, dense_in), hop("ch", 1, dense_out)
    sent, first_weight, second_weight, first_bias = lax.optimization_barrier(
        (sent, first_weight, second_weight, first_bias)
    )
    w1, w2 = big_weight(first_weight), big_weight(second_weight)
    b1 = lane_order(first_bias.reshape(1, -1), 1, sz.chans)
    got = swap_modes(sent)
    sent, spec, act, slope = call(
        bind(mix_kernel),
        (message, flat, flat, flat),
        [scr, flat_scr],
        (got, cs, cs_t, w1, b1, w2),
        10,
        after=(*up_parts, far_in),
    )
    got = swap_modes(sent)
    wins = (dense_in, near_in, far_in, hop("ch", 1, far_in))
    wouts = (dense_out, near_out, far_out, hop("ch", 1, far_out))
    tokens = sz.own * sz.lon_pad
    grown = array(bf16, tokens, width)
    hidden = array(bf16, n_ch, tokens, hid)
    sent, sg, mid, upf, hidden_act, hidden_grad, sent_part = call(
        bind(mlp_kernel),
        (message, array(f32, *cells), grown, grown, hidden, hidden, array(bf16, n_ch // 2, 2, hid, width)),
        [
            scr,
            pltpu.VMEM(cells, f32),
            pltpu.VMEM(grown.shape, f32),
            pltpu.VMEM((sz.own, sz.lon, LANES), f32),
            pltpu.VMEM(cells, bf16),
        ],
        (at, got, x, inverse_2, inverse_t, cotangent, *up_parts, *wins, *wouts),
        20,
        1,
    )
    got = swap_modes(sent)
    factors = (at, mid, upf, hidden_act, hidden_grad)
    got_part = hop("ch", 1, sent_part)
    a_keep, a_send, b_keep, b_send = call(
        bind(dense_keep_kernel),
        split(hid, width) + split(2, hid // 2, width),
        [pltpu.VMEM((hid, width), f32)],
        (*factors, got_part),
        0,
        1,
    )
    eight = n_sp == 8
    small_rows = up_to(sz.chans // 2 + 1, 16)
    before = (a_keep,)
    if eight:
        a_got, b_got = hop("ch", 2, a_send), hop("sp", 1, b_send)
        a_keep, a_send, b_keep, b_send = before = call(
            bind(dense_step_kernel),
            split(hid // 2, width) * 2,
            [pltpu.VMEM((hid, width), f32)],
            (at, a_keep, a_got, b_keep, b_got),
            0,
            1,
        )
        a_got, b_got = hop("sp", 1, a_send), hop("ch", 2, b_send)
    dmix, dpre = call(
        bind(mix_back_kernel), (flat, flat), [scr], (got, cs, w2.T, slope), 6, after=before[:1]
    )
    parts = n_sp // 2
    piece = 2 * hid // n_sp
    back_args = (dpre, cs_t, w1.T)
    if eight:
        sent, keep, send = call(
            bind(spectrum_back_cut_kernel),
            (message,) + split(2, piece, width),
            [scr, flat_scr, pltpu.VMEM((parts, piece, width), f32)],
            (at, *back_args, a_keep, a_got, b_keep, b_got),
            6,
            1,
        )
        got_near = hop("sp", 2, send)
    else:
        sent = call(bind(spectrum_back_kernel), message, [scr, flat_scr], back_args, 6)
    got = swap_modes(sent)
    last = ()
    smalls = (spec, dpre, act, dmix)
    if eight:
        small = call(
            bind(small_round_kernel),
            array(bf16, small_rows, width),
            [pltpu.VMEM((small_rows, width), f32)],
            smalls,
            0,
            after=(keep,),
        )
        small_got = hop("sp", 1, small)
        own, send = call(bind(far_cut_kernel), split(piece, width), [], (at, keep, got_near), 0, 1)
        got_far = hop("sp", 4, send)
        last = (own, small_got)
    grads = call(
        bind(field_kernel),
        [array(bf16, *cells[1:])] * n_ch,
        [scr, pltpu.VMEM(cells, bf16)],
        (at, got, x, sg, forward_t),
        6,
        1,
        after=last,
    )
    grad_parts = [grads[0]] + [hop("ch", d, grads[d]) for d in range(1, n_ch)]
    w_shapes = [array(f32, *first_weight.shape)] * 2 + [array(f32, 1, 2 * sz.chans)]
    if eight:
        block = call(bind(block_kernel), array(bf16, piece, width), [], (own, got_far), 0, after=(grads[0],))
        near = [hop("sp", 2 * d, block) for d in range(1, parts)]
        far_own = hop("sp", 1, block)
        small_shape = array(bf16, small_rows, width)
        small = call(bind(block_kernel), small_shape, [], (small, small_got), 0)
        small_got = hop("sp", 2, small)
        stacked = call(
            bind(stack_kernel), array(bf16, parts - 1, piece, width), [], near, 0, after=(*grad_parts[1:], small_got, far_own)
        )
        far = hop("sp", 1, stacked)
        small = call(bind(block_kernel), small_shape, [], (small, small_got), 0)
        in_grad, out_grad, w1_grad, w2_grad, b1_grad = call(
            bind(place_kernel),
            [array(bf16, width, hid), array(bf16, hid, width)] + w_shapes,
            [pltpu.VMEM((small_rows, width), f32)],
            (at, small, hop("sp", 4, small), far, far_own, block, *near),
            0,
            1,
        )
    else:
        high = (ch_at // 2 == 1)
        b_full = b_whole(b_keep, b_send, sp_at)
        in_grad = a_keep + hop("ch", 2, a_send).astype(f32)
        out_keep = jnp.where(high, b_full[1], b_full[0])
        out_grad = out_keep + hop("ch", 2, jnp.where(high, b_full[0], b_full[1]))
        small = call(bind(small_kernel), array(f32, small_rows, width), [], smalls, 0)
        in_grad, out_grad, small = lax.psum((in_grad, out_grad, small), "sp")
        half = width // 2
        in_grad = jnp.concatenate([in_grad[:, :half], in_grad[:, half:]], axis=0).astype(bf16)
        out_grad = out_grad.astype(bf16)
        w1_grad, w2_grad, b1_grad = call(bind(spread_small), w_shapes, [], (small,), 0)
    grad = call(bind(join_kernel), array(bf16, n_ch * sz.own, *cells[2:]), [], (at, *grad_parts), 0, 1)
    return (grad[: sz.rows], w1_grad, b1_grad.reshape(first_bias.shape), w2_grad, in_grad, out_grad)


def solution(mesh):
    placed = (
        P("sp", None, "ch"),
        P("sp", None, "ch"),
        P(None, "ch", None, None),
        P(None, "ch", None),
        P(None, "ch", None, None),
        P(None, "ch"),
        P("ch", None),
    )
    return jax.shard_map(
        local,
        mesh=mesh,
        in_specs=placed,
        out_specs=(
            P("sp", None, "ch"),
            P(None, "ch", None, None),
            P(None, "ch", None),
            P(None, "ch", None, None),
            P(None, "ch"),
            P("ch", None),
        ),
        check_vma=False,
    )
```

```python
import math

import jax
import jax.numpy as jnp
import ml_dtypes
import numpy as np
from jax import lax
from jax.experimental import pallas as pl
from jax.experimental.pallas import tpu as pltpu
from jax.sharding import PartitionSpec as P

LAT = 90
BAND_MAX = 16
LANES = 128
HALF = 64

eps = 1e-05
f32 = jnp.float32
bf16 = jnp.bfloat16
HIGH = lax.Precision.HIGH
VMEM_BYTES = 50 * 2**20


def up_to(value, step):
    return (value + step - 1) // step * step


class Sizes:
    def __init__(self, block, n_sp, n_ch):
        self.rows, self.lon, self.chans = block
        self.n_sp, self.n_ch = n_sp, n_ch
        self.width = self.chans * n_ch
        self.own = -(-self.rows // n_ch)
        self.bands = min(BAND_MAX, n_sp)
        self.samples = n_sp // self.bands
        self.modes = -(-(self.lon // 2 + 1) // n_sp)
        self.all_modes = self.modes * n_sp
        self.parts = 2 * self.chans // LANES
        self.pad = up_to(self.parts * self.own * self.modes, 16)
        self.sources = self.bands * n_ch
        self.lat_in = self.own * self.sources
        self.lat_modes = up_to(LAT, 16)
        self.planes = self.samples * self.modes
        self.lon_pad = up_to(self.lon, 16)

    def slot(self, q, r, m):
        return (q * self.own + r) * self.modes + m


def lon_tables(sz):
    mode = (np.arange(sz.n_sp)[None, :] * sz.modes + np.arange(sz.modes)[:, None]).reshape(-1, 1)
    cell = np.arange(sz.lon)[None, :]
    phase = 2.0 * np.pi / sz.lon * (mode * cell % sz.lon)
    live = (mode <= sz.lon // 2).astype(np.float64)
    inner = ((mode > 0) & (mode < sz.lon // 2)).astype(np.float64)
    scale = 1.0 / math.sqrt(sz.lon)
    cosine = np.cos(phase) * live * scale
    sine = np.sin(phase) * inner * scale
    forward = np.concatenate([cosine, -sine], axis=0)
    inverse = np.concatenate([cosine * (live + inner), -2.0 * sine], axis=0).T
    return forward.astype(np.float32), np.ascontiguousarray(inverse).astype(np.float32)


def lat_table(sz):
    r = np.arange(sz.own)[:, None, None]
    band = np.arange(sz.bands)[None, :, None]
    c = np.arange(sz.n_ch)[None, None, :]
    cell = band * sz.rows + c * sz.own + r
    live = np.logical_and(c * sz.own + r < sz.rows, cell < LAT).reshape(1, -1)
    cell = cell.reshape(1, -1)
    mode = np.arange(sz.lat_modes)[:, None]
    live = np.logical_and(live, mode < LAT) / math.sqrt(LAT)
    phase = 2.0 * np.pi / LAT * (mode * cell % LAT)
    return (
        (np.cos(phase) * live).astype(np.float32),
        (np.sin(phase) * live).astype(np.float32),
    )


def gelu(v):
    return v * (0.5 * (1.0 + lax.erf(v * np.float32(math.sqrt(0.5)))))


def gelu_pair(v):
    cdf = 0.5 * (1.0 + lax.erf(v * np.float32(math.sqrt(0.5))))
    pdf = jnp.exp(-0.5 * v * v) * np.float32(1.0 / math.sqrt(2.0 * math.pi))
    return v * cdf, cdf + v * pdf


def mm(a, b, precision=HIGH):
    return jnp.dot(a, b, precision=precision, preferred_element_type=f32)


def two_terms(table, rows):
    table = np.pad(table, ((0, rows - table.shape[0]), (0, 0)))
    first = table.astype(ml_dtypes.bfloat16)
    second = (table - first.astype(np.float32)).astype(ml_dtypes.bfloat16)
    return jnp.asarray(np.concatenate([first, second], axis=0))


def mm_two(table, values):
    y = jnp.dot(table, values.astype(bf16), preferred_element_type=f32)
    n = table.shape[0] // 2
    return y[:n] + y[n:]


def swap(values):
    lane = lax.broadcasted_iota(jnp.int32, values.shape, 1)
    turned = pltpu.roll(values, HALF, 1)
    return jnp.where(lane < HALF, turned, -turned)


def store_modes(sz, scr, y, r, c):
    n = sz.all_modes
    re, im = y[:n], y[n:]
    pieces = (re[:, :LANES], im[:, :LANES], re[:, LANES:] + pltpu.roll(im[:, LANES:], HALF, 1))
    for q, piece in enumerate(pieces):
        for m in range(sz.modes):
            scr[pl.ds(c * sz.pad + sz.slot(q, r, m), sz.n_sp, stride=sz.n_ch * sz.pad), :] = piece[
                m * sz.n_sp : (m + 1) * sz.n_sp
            ]


def load_modes(sz, scr, r, c):
    q0, q1, q2 = (
        jnp.concatenate(
            [
                scr[pl.ds(c * sz.pad + sz.slot(q, r, m), sz.n_sp, stride=sz.n_ch * sz.pad), :]
                for m in range(sz.modes)
            ],
            axis=0,
        )
        for q in range(3)
    )
    left = jnp.concatenate([q0, q1], axis=0)
    right = jnp.concatenate([q2, pltpu.roll(q2, HALF, 1)], axis=0)
    return jnp.concatenate([left, right], axis=1)


def wide(values):
    rows, lanes = values.shape
    return jnp.concatenate([values, jnp.zeros((rows, up_to(lanes, LANES) - lanes), f32)], axis=1)


def plane_start(sz, s, q, r, m):
    return s * sz.sources * sz.pad + sz.slot(q, r, m)


def center_scale(chunks, width):
    mean = sum(jnp.sum(v, axis=-1, keepdims=True) for v in chunks) / width
    chunks = [v - mean for v in chunks]
    var = sum(jnp.sum(v * v, axis=-1, keepdims=True) for v in chunks) / width
    recip = lax.rsqrt(var + eps)
    return [v * recip for v in chunks], recip


def norm_back(normed, recip, incoming, width):
    first = sum(jnp.sum(g, axis=-1, keepdims=True) for g in incoming) / width
    second = sum(jnp.sum(g * z, axis=-1, keepdims=True) for g, z in zip(incoming, normed)) / width
    return [recip * (g - first - z * second) for g, z in zip(incoming, normed)]


def gather_parts(sz, at_ref, own_ref, parts, out_ref):
    me = at_ref[4]
    for r in range(sz.own):
        out_ref[me, r] = own_ref[me * sz.own + r]
    for d, part in enumerate(parts):
        out_ref[me ^ (d + 1)] = part[...]


def norm_spectrum_kernel(sz, at_ref, *refs):
    own_ref, *parts = refs[: sz.n_ch]
    tab_ref, out_ref, x_ref, scr = refs[sz.n_ch :]
    gather_parts(sz, at_ref, own_ref, parts, x_ref)
    for r in range(sz.own):
        normed, _ = center_scale([x_ref[c, r].astype(f32) for c in range(sz.n_ch)], sz.width)
        for c in range(sz.n_ch):
            store_modes(sz, scr, mm(tab_ref[...], wide(normed[c])), r, c)
    out_ref[...] = scr[...].astype(bf16)


def lat_forward(sz, scr, cs, p):
    s, m = divmod(p, sz.modes)
    x0, x1, x2 = (
        jnp.concatenate(
            [
                scr[pl.ds(plane_start(sz, s, q, r, m), sz.sources, stride=sz.pad), :]
                for r in range(sz.own)
            ],
            axis=0,
        )
        for q in range(3)
    )
    both = jnp.concatenate(
        [jnp.concatenate([x0, x1, x2], axis=1), jnp.concatenate([x1, -x0, swap(x2)], axis=1)], axis=0
    )
    return mm_two(cs, both)


def lat_inverse(sz, scr, cs_t, o, p):
    s, m = divmod(p, sz.modes)
    o0, o1, o2 = (o[:, q * LANES : (q + 1) * LANES] for q in range(3))
    both = jnp.concatenate(
        [jnp.concatenate([o0, o1, o2], axis=1), jnp.concatenate([-o1, o0, -swap(o2)], axis=1)], axis=0
    )
    y = mm_two(cs_t, both)
    for q in range(3):
        for r in range(sz.own):
            scr[pl.ds(plane_start(sz, s, q, r, m), sz.sources, stride=sz.pad), :] = y[
                r * sz.sources : (r + 1) * sz.sources, q * LANES : (q + 1) * LANES
            ]


def mix_kernel(sz, in_ref, cs_ref, cst_ref, w1_ref, b1_ref, w2_ref, out_ref, scr, spec, mixed):
    n = sz.lat_modes
    scr[...] = in_ref[...].astype(f32)
    for p in range(sz.planes):
        spec[p * n : (p + 1) * n, :] = lat_forward(sz, scr, cs_ref[...], p)

    def block(i, carry):
        rows = pl.ds(pl.multiple_of(i * 2 * n, 16), 2 * n)
        mixed[rows, :] = mm(gelu(mm(spec[rows, :], w1_ref[...]) + b1_ref[...]), w2_ref[...])
        return carry

    lax.fori_loop(0, sz.planes // 2, block, 0)
    for p in range(sz.planes):
        lat_inverse(sz, scr, cst_ref[...], mixed[p * n : (p + 1) * n, :], p)
    out_ref[...] = scr[...].astype(bf16)


def mix_save_kernel(sz, in_ref, cs_ref, w1_ref, b1_ref, spec_ref, act_ref, slope_ref, scr):
    n = sz.lat_modes
    scr[...] = in_ref[...].astype(f32)
    for p in range(sz.planes):
        spec_ref[p * n : (p + 1) * n, :] = lat_forward(sz, scr, cs_ref[...], p)

    def block(i, carry):
        rows = pl.ds(pl.multiple_of(i * 2 * n, 16), 2 * n)
        act, slope = gelu_pair(mm(spec_ref[rows, :], w1_ref[...]) + b1_ref[...])
        act_ref[rows, :] = act
        slope_ref[rows, :] = slope
        return carry

    lax.fori_loop(0, sz.planes // 2, block, 0)


def mix_back_kernel(sz, in_ref, cs_ref, w2t_ref, slope_ref, dmix_ref, dpre_ref, scr):
    n = sz.lat_modes
    scr[...] = in_ref[...].astype(f32)
    for p in range(sz.planes):
        dmix_ref[p * n : (p + 1) * n, :] = lat_forward(sz, scr, cs_ref[...], p)

    def block(i, carry):
        rows = pl.ds(pl.multiple_of(i * 2 * n, 16), 2 * n)
        dpre_ref[rows, :] = mm(dmix_ref[rows, :], w2t_ref[...]) * slope_ref[rows, :]
        return carry

    lax.fori_loop(0, sz.planes // 2, block, 0)


def spectrum_back_cut_kernel(sz, at_ref, dpre_ref, cst_ref, w1t_ref, *refs):
    near_cut_kernel(sz, at_ref, *refs[:4], *refs[5:7], refs[9])
    spectrum_back_kernel(sz, dpre_ref, cst_ref, w1t_ref, refs[4], *refs[7:9])


def spectrum_back_kernel(sz, dpre_ref, cst_ref, w1t_ref, out_ref, scr, dspec):
    n = sz.lat_modes

    def block(i, carry):
        rows = pl.ds(pl.multiple_of(i * 2 * n, 16), 2 * n)
        dspec[rows, :] = mm(dpre_ref[rows, :], w1t_ref[...])
        return carry

    lax.fori_loop(0, sz.planes // 2, block, 0)
    for p in range(sz.planes):
        lat_inverse(sz, scr, cst_ref[...], dspec[p * n : (p + 1) * n, :], p)
    out_ref[...] = scr[...].astype(bf16)


def mlp_kernel(sz, at_ref, in_ref, x_ref, inv_ref, invt_ref, *refs):
    n = sz.n_ch
    own_ref, *parts = refs[:n]
    win_refs, wout_refs = refs[n : 2 * n], refs[2 * n : 3 * n]
    out_ref, sg_ref, mid_ref, upf_ref, act_ref, hg_ref, part_ref, scr, z_scr, mg_scr, rs_scr, up_ref = refs[3 * n :]
    me, first_row = at_ref[4], at_ref[5]
    gather_parts(sz, at_ref, own_ref, parts, up_ref)
    for r in range(sz.own):

        def mask(r=r):
            for c in range(n):
                up_ref[c, r] = jnp.zeros((sz.lon, sz.chans), bf16)

        pl.when(first_row + r >= LAT)(mask)
    scr[...] = in_ref[...].astype(f32)
    mid_ref[...] = jnp.zeros(mid_ref.shape, bf16)
    upf_ref[...] = jnp.zeros(upf_ref.shape, bf16)
    c_all = range(sz.n_ch)

    def place(r, c):
        return (slice(r * sz.lon_pad, r * sz.lon_pad + sz.lon), slice(c * sz.chans, (c + 1) * sz.chans))

    for r in range(sz.own):
        xs = [x_ref[c, r].astype(f32) for c in c_all]
        normed, _ = center_scale(xs, sz.width)
        summed = [
            xs[c] + normed[c] + mm_two(inv_ref[...], load_modes(sz, scr, r, c))[: sz.lon, : sz.chans] for c in c_all
        ]
        zs, recip = center_scale(summed, sz.width)
        rs_scr[r] = jnp.broadcast_to(recip, (sz.lon, LANES))
        for c in c_all:
            z_scr[c, r] = zs[c]
            mid_ref[place(r, c)] = zs[c].astype(bf16)
            upf_ref[place(r, c)] = up_ref[c, r]
    mg_scr[...] = jnp.zeros(mg_scr.shape, f32)
    nt = (((1,), (1,)), ((), ()))

    for d in range(n):
        j = me ^ d
        pre = mm(mid_ref[...], win_refs[d][...], None)
        back = lax.dot_general(upf_ref[...], wout_refs[d][...], nt, preferred_element_type=f32)
        act, slope = gelu_pair(pre)
        act_ref[j] = act.astype(bf16)
        grad = (back * slope).astype(bf16)
        hg_ref[j] = grad
        mg_scr[...] += lax.dot_general(grad, win_refs[d][...], nt, preferred_element_type=f32)
        if d % 2:
            dense_parts(sz, part_ref, at_ref[1] ^ (d // 2), j, mid_ref, upf_ref, act_ref, hg_ref)
    for r in range(sz.own):
        zs = [z_scr[c, r] for c in c_all]
        grads = norm_back(zs, rs_scr[r][:, :1], [mg_scr[place(r, c)] for c in c_all], sz.width)
        for c in c_all:
            total = up_ref[c, r].astype(f32) + grads[c]
            sg_ref[c, r] = total
            store_modes(sz, scr, mm(invt_ref[...], wide(total)), r, c)
    out_ref[...] = scr[...].astype(bf16)


def field_kernel(sz, at_ref, in_ref, x_ref, sg_ref, fwdt_ref, *refs):
    outs, (scr, out_scr) = refs[: sz.n_ch], refs[sz.n_ch :]
    scr[...] = in_ref[...].astype(f32)
    c_all = range(sz.n_ch)
    for r in range(sz.own):
        normed, recip = center_scale([x_ref[c, r].astype(f32) for c in c_all], sz.width)
        sg = [sg_ref[c, r] for c in c_all]
        incoming = [sg[c] + mm_two(fwdt_ref[...], load_modes(sz, scr, r, c))[: sz.lon, : sz.chans] for c in c_all]
        grads = norm_back(normed, recip, incoming, sz.width)
        for c in c_all:
            out_scr[c, r] = (sg[c] + grads[c]).astype(bf16)
    for d, out in enumerate(outs):
        out[...] = out_scr[at_ref[4] ^ d]


def join_kernel(sz, at_ref, *refs):
    parts, out_ref = refs[:-1], refs[-1]
    for d, part in enumerate(parts):
        for r in range(sz.own):
            out_ref[(at_ref[4] ^ d) * sz.own + r] = part[r]


def dense_keep_kernel(sz, at_ref, mid_ref, upf_ref, act_ref, hg_ref, got_ref,
                      a_keep, a_send, b_keep, b_send, scr):
    low, high, x = at_ref[0], at_ref[1], at_ref[2]
    tn = (((0,), (0,)), ((), ()))
    half = sz.width // 2
    for k, out in ((high, a_keep), (1 - high, a_send)):
        for side in range(2):
            lanes = slice(side * half, (side + 1) * half)
            part = lax.dot_general(mid_ref[:, lanes], hg_ref[2 * k + low], tn, preferred_element_type=f32)
            out[:, lanes] = (part + got_ref[k, 0, :, lanes].astype(f32)).astype(out.dtype)
    rows = scr.shape[0] // 2
    for k in range(2):
        part = lax.dot_general(act_ref[2 * k + low], upf_ref[...], tn, preferred_element_type=f32)
        scr[...] = part + got_ref[k, 1].astype(f32)
        b_keep[k] = scr[pl.ds(pl.multiple_of(x * rows, 16), rows), :]
        b_send[k] = scr[pl.ds(pl.multiple_of((1 - x) * rows, 16), rows), :].astype(bf16)


def lane_runs(p, b, size):
    if b == 0:
        return [(p * LANES, p * LANES + size)]
    return [(p * LANES + size, (p + 1) * LANES), (2 * LANES + p * HALF, 2 * LANES + (p + 1) * HALF)]


def take(values, p, b, size, axis):
    pieces = [lax.slice_in_dim(values, i, j, axis=axis) for i, j in lane_runs(p, b, size)]
    return pieces[0] if len(pieces) == 1 else jnp.concatenate(pieces, axis=axis)


def dense_step_kernel(sz, at_ref, a_keep, a_got, b_keep, b_got, a2_keep, a2_send, b2_keep, b2_send, scr):
    high, x = at_ref[1], at_ref[2]
    rows = a2_keep.shape[0]
    scr[...] = a_keep[...] + a_got[...].astype(f32)
    a2_keep[...] = scr[pl.ds(pl.multiple_of(x * rows, 16), rows), :]
    a2_send[...] = scr[pl.ds(pl.multiple_of((1 - x) * rows, 16), rows), :].astype(bf16)
    b2_keep[...] = b_keep[high] + b_got[high].astype(f32)
    b2_send[...] = (b_keep[1 - high] + b_got[1 - high].astype(f32)).astype(bf16)


def near_cut_kernel(sz, at_ref, a_keep, a_got, b_keep, b_got, keep, send, cut):
    low = at_ref[3] % 2
    many = cut.shape[1] // 2
    for p in range(cut.shape[0]):
        rows = slice(p * many, (p + 1) * many)
        cut[p, 0:many] = a_keep[rows, :] + a_got[rows, :].astype(f32)
        cut[p, many : 2 * many] = b_keep[rows, :] + b_got[rows, :].astype(f32)
    for h in range(2):
        keep[h] = cut[2 * h + low]
        send[h] = cut[2 * h + 1 - low].astype(bf16)


def far_cut_kernel(sz, at_ref, keep, got, own, send):
    high = at_ref[3] // 2
    own[...] = keep[high] + got[high].astype(f32)
    send[...] = (keep[1 - high] + got[1 - high].astype(f32)).astype(bf16)


def stack_kernel(sz, *refs):
    for i, ref in enumerate(refs[:-1]):
        refs[-1][i] = ref[...]


def block_kernel(sz, own, *refs):
    parts, out_ref = refs[:-1], refs[-1]
    total = own[...].astype(f32)
    for part in parts:
        total = total + part[...].astype(f32)
    out_ref[...] = total.astype(bf16)


def small_kernel(sz, spec_ref, dpre_ref, act_ref, dmix_ref, out_ref):
    tn = (((0,), (0,)), ((), ()))
    size = sz.chans // 2
    out_ref[...] = jnp.zeros(out_ref.shape, f32)
    for g, (left, right) in enumerate(((spec_ref, dpre_ref), (act_ref, dmix_ref))):
        big = lax.dot_general(left[...], right[...], tn, precision=HIGH, preferred_element_type=f32)
        for b in range(2):
            rows = [take(big, p, b, size, 0) for p in range(2)]
            real = take(rows[0], 0, b, size, 1) + take(rows[1], 1, b, size, 1)
            imag = take(rows[0], 1, b, size, 1) - take(rows[1], 0, b, size, 1)
            for p, value in enumerate((real, imag)):
                k = (g * 2 + p) * 2 + b
                out_ref[0:size, k * size : (k + 1) * size] = value
    bias = jnp.sum(dpre_ref[...], axis=0, keepdims=True)
    for p in range(2):
        for b in range(2):
            k = p * 2 + b
            out_ref[size : size + 1, k * size : (k + 1) * size] = take(bias, p, b, size, 1)


def small_round_kernel(sz, *refs):
    out_ref, scr = refs[4:]
    small_kernel(sz, *refs[:4], scr)
    out_ref[...] = scr[...].astype(bf16)


def place_kernel(sz, at_ref, s_own, s_far, far, far_own, *refs):
    parts = sz.n_sp // 2
    near, (in_ref, out_ref, w1_ref, w2_ref, b1_ref, scr) = refs[:parts], refs[parts:]
    many = far.shape[1] // 2
    half = sz.width // 2
    x = at_ref[2]
    for i in range(2 * parts):
        ref = near[i] if i < parts else far_own if i == parts else far.at[i - parts - 1]
        place = (x ^ (i // parts)) * parts + (at_ref[3] ^ (i % parts))
        base = pl.multiple_of(place * many, 16)
        in_ref[pl.ds(base, many), :] = ref[0:many, 0:half]
        in_ref[pl.ds(base + half, many), :] = ref[0:many, half : 2 * half]
        out_ref[pl.ds(base, many), :] = ref[many:, :]
    scr[...] = s_own[...].astype(f32) + s_far[...].astype(f32)
    spread_small(sz, scr, w1_ref, w2_ref, b1_ref)


def spread_small(sz, scr, w1_ref, w2_ref, b1_ref):
    size = sz.chans // 2
    for g, out in enumerate((w1_ref, w2_ref)):
        for p in range(2):
            for b in range(2):
                k = (g * 2 + p) * 2 + b
                out[p, b] = scr[0:size, k * size : (k + 1) * size]
    b1_ref[...] = scr[size : size + 1, 0 : 4 * size]


def call(body, outs, scratch, args, micros, scalars=0, after=()):
    in_specs = [pl.BlockSpec(memory_space=pltpu.SMEM)] * scalars
    in_specs += [pl.BlockSpec(memory_space=pltpu.VMEM)] * (len(args) - scalars)
    in_specs += [pl.BlockSpec(memory_space=pl.ANY)] * len(after)
    n_args, n_after = len(args), len(after)

    def wrapped(*refs):
        body(*refs[:n_args], *refs[n_args + n_after :])

    return pl.pallas_call(
        wrapped,
        in_specs=in_specs,
        out_shape=outs,
        scratch_shapes=scratch,
        compiler_params=pltpu.CompilerParams(vmem_limit_bytes=VMEM_BYTES),
        cost_estimate=pl.CostEstimate(flops=micros * 10**9, bytes_accessed=2**20, transcendentals=0),
    )(*args, *after)


def block_diagonal(weight):
    blocks, size = weight.shape[0], weight.shape[1]
    ident = jnp.eye(blocks, dtype=f32)
    return jnp.einsum("be,bio->bieo", ident, weight).reshape(blocks * size, blocks * size)


def lane_order(values, axis, chans):
    def cut(a, b):
        return lax.slice_in_dim(values, a, b, axis=axis)
    return jnp.concatenate(
        [cut(0, LANES), cut(chans, chans + LANES), cut(LANES, chans), cut(chans + LANES, 2 * chans)], axis=axis
    )


def natural_order(values, axis, chans):
    def cut(a, b):
        return lax.slice_in_dim(values, a, b, axis=axis)
    rest = chans - LANES
    return jnp.concatenate(
        [cut(0, LANES), cut(2 * LANES, 2 * LANES + rest), cut(LANES, 2 * LANES), cut(2 * LANES + rest, 2 * chans)],
        axis=axis,
    )


def big_weight(weight):
    real, imag = block_diagonal(weight[0]), block_diagonal(weight[1])
    full = jnp.concatenate(
        [jnp.concatenate([real, imag], axis=1), jnp.concatenate([-imag, real], axis=1)], axis=0
    )
    chans = real.shape[0]
    return lane_order(lane_order(full, 0, chans), 1, chans)


def small_grad(big, blocks):
    chans = big.shape[0] // 2
    size = chans // blocks
    full = natural_order(natural_order(big, 0, chans), 1, chans)
    full = full.reshape(2, blocks, size, 2, blocks, size)
    diag = jnp.stack([full[:, b, :, :, b, :] for b in range(blocks)], axis=0)
    real = diag[:, 0, :, 0] + diag[:, 1, :, 1]
    imag = diag[:, 0, :, 1] - diag[:, 1, :, 0]
    return jnp.stack([real, imag], axis=0)


def hop(axis, distance, values):
    n = lax.axis_size(axis)
    return lax.ppermute(values, axis, [(i, i ^ distance) for i in range(n)])


def dense_parts(sz, out_ref, k, j, mid_ref, upf_ref, act_ref, hg_ref):
    tn = (((0,), (0,)), ((), ()))
    half = sz.width // 2
    for side in range(2):
        lanes = slice(side * half, (side + 1) * half)
        out_ref[k, 0, :, lanes] = lax.dot_general(
            mid_ref[:, lanes], hg_ref[j], tn, preferred_element_type=f32
        ).astype(out_ref.dtype)
    out_ref[k, 1] = lax.dot_general(act_ref[j], upf_ref[...], tn, preferred_element_type=f32).astype(out_ref.dtype)


def b_whole(keep, send, sp_at):
    odd = sp_at % 2 == 1
    send = send.astype(f32)
    return jnp.concatenate([jnp.where(odd, send, keep), jnp.where(odd, keep, send)], axis=1)


def array(dtype, *shape):
    return jax.ShapeDtypeStruct(shape, dtype)


def split(*shape):
    return array(f32, *shape), array(bf16, *shape)


def local(field, cotangent, first_weight, first_bias, second_weight, dense_in, dense_out):
    n_sp, n_ch = lax.axis_size("sp"), lax.axis_size("ch")
    sz = Sizes(field.shape, n_sp, n_ch)
    both = ("sp", "ch")
    hid, width = dense_in.shape[1], sz.width
    forward, inverse = lon_tables(sz)
    forward_t, inverse_2 = two_terms(forward.T, sz.lon_pad), two_terms(inverse, sz.lon_pad)
    forward, inverse_t = jnp.asarray(forward), jnp.asarray(inverse.T)
    cosine, sine = lat_table(sz)
    cs = two_terms(np.concatenate([cosine, sine], axis=1), sz.lat_modes)
    cs_t = two_terms(np.concatenate([cosine.T, sine.T], axis=1), sz.lat_in)
    sp_at, ch_at = lax.axis_index("sp"), lax.axis_index("ch")
    first_row = sp_at % sz.bands * sz.rows + ch_at * sz.own
    at = jnp.stack([ch_at % 2, ch_at // 2, sp_at % 2, sp_at // 2, ch_at, first_row]).astype(jnp.int32)
    extra = sz.own * n_ch - sz.rows
    if extra:
        field, cotangent = (jnp.pad(v, ((0, extra), (0, 0), (0, 0))) for v in (field, cotangent))

    def row_parts(values):
        got = {}
        for d in reversed(range(1, n_ch)):
            got[d] = hop("ch", d, lax.dynamic_slice_in_dim(values, (ch_at ^ d) * sz.own, sz.own, 0))
        return [got[d] for d in range(1, n_ch)]

    def swap_modes(message):
        message = message.reshape(n_sp * n_ch, sz.pad, LANES)
        message = lax.all_to_all(message, both, split_axis=0, concat_axis=0, tiled=True)
        return message.reshape(n_sp * n_ch * sz.pad, LANES)

    def bind(kernel):
        return lambda *refs: kernel(sz, *refs)

    message = array(bf16, n_sp * n_ch * sz.pad, LANES)
    scr = pltpu.VMEM(message.shape, f32)
    flat = array(f32, sz.planes * sz.lat_modes, 2 * sz.chans)
    flat_scr = pltpu.VMEM(flat.shape, f32)
    cells = (n_ch, sz.own, sz.lon, sz.chans)

    x_parts = row_parts(field)
    x_parts, cotangent, dense_in, dense_out = lax.optimization_barrier((x_parts, cotangent, dense_in, dense_out))
    sent, x = call(
        bind(norm_spectrum_kernel), (message, array(bf16, *cells)), [scr], (at, field, *x_parts, forward), 3, 1
    )
    up_parts = row_parts(cotangent)
    far_in, far_out = hop("ch", 2, dense_in), hop("ch", 2, dense_out)
    near_in, near_out = hop("ch", 1, dense_in), hop("ch", 1, dense_out)
    sent, first_weight, second_weight, first_bias = lax.optimization_barrier(
        (sent, first_weight, second_weight, first_bias)
    )
    w1, w2 = big_weight(first_weight), big_weight(second_weight)
    b1 = lane_order(first_bias.reshape(1, -1), 1, sz.chans)
    got = swap_modes(sent)
    modes_in = got
    sent = call(
        bind(mix_kernel),
        message,
        [scr, flat_scr, flat_scr],
        (modes_in, cs, cs_t, w1, b1, w2),
        10,
        after=(far_in, far_out),
    )
    got = swap_modes(sent)
    spec, act, slope = call(
        bind(mix_save_kernel), (flat, flat, flat), [scr], (modes_in, cs, w1, b1), 30, after=(sent,)
    )
    wins = (dense_in, near_in, far_in, hop("ch", 1, far_in))
    wouts = (dense_out, near_out, far_out, hop("ch", 1, far_out))
    tokens = sz.own * sz.lon_pad
    grown = array(bf16, tokens, width)
    hidden = array(bf16, n_ch, tokens, hid)
    sent, sg, mid, upf, hidden_act, hidden_grad, sent_part = call(
        bind(mlp_kernel),
        (message, array(f32, *cells), grown, grown, hidden, hidden, array(bf16, n_ch // 2, 2, hid, width)),
        [
            scr,
            pltpu.VMEM(cells, f32),
            pltpu.VMEM(grown.shape, f32),
            pltpu.VMEM((sz.own, sz.lon, LANES), f32),
            pltpu.VMEM(cells, bf16),
        ],
        (at, got, x, inverse_2, inverse_t, cotangent, *up_parts, *wins, *wouts),
        20,
        1,
        after=(slope,),
    )
    got = swap_modes(sent)
    factors = (at, mid, upf, hidden_act, hidden_grad)
    got_part = hop("ch", 1, sent_part)
    a_keep, a_send, b_keep, b_send = call(
        bind(dense_keep_kernel),
        split(hid, width) + split(2, hid // 2, width),
        [pltpu.VMEM((hid, width), f32)],
        (*factors, got_part),
        0,
        1,
    )
    eight = n_sp == 8
    small_rows = up_to(sz.chans // 2 + 1, 16)
    before = (a_keep,)
    if eight:
        a_got, b_got = hop("ch", 2, a_send), hop("sp", 1, b_send)
        a_keep, a_send, b_keep, b_send = before = call(
            bind(dense_step_kernel),
            split(hid // 2, width) * 2,
            [pltpu.VMEM((hid, width), f32)],
            (at, a_keep, a_got, b_keep, b_got),
            0,
            1,
        )
        a_got, b_got = hop("sp", 1, a_send), hop("ch", 2, b_send)
    dmix, dpre = call(
        bind(mix_back_kernel), (flat, flat), [scr], (got, cs, w2.T, slope), 6, after=before[:1]
    )
    parts = n_sp // 2
    piece = 2 * hid // n_sp
    back_args = (dpre, cs_t, w1.T)
    if eight:
        sent, keep, send = call(
            bind(spectrum_back_cut_kernel),
            (message,) + split(2, piece, width),
            [scr, flat_scr, pltpu.VMEM((parts, piece, width), f32)],
            (at, *back_args, a_keep, a_got, b_keep, b_got),
            6,
            1,
        )
        got_near = hop("sp", 2, send)
    else:
        sent = call(bind(spectrum_back_kernel), message, [scr, flat_scr], back_args, 6)
    got = swap_modes(sent)
    last = ()
    smalls = (spec, dpre, act, dmix)
    if eight:
        small = call(
            bind(small_round_kernel),
            array(bf16, small_rows, width),
            [pltpu.VMEM((small_rows, width), f32)],
            smalls,
            0,
            after=(keep,),
        )
        small_got = hop("sp", 1, small)
        own, send = call(bind(far_cut_kernel), split(piece, width), [], (at, keep, got_near), 0, 1)
        got_far = hop("sp", 4, send)
        last = (own, small_got)
    grads = call(
        bind(field_kernel),
        [array(bf16, *cells[1:])] * n_ch,
        [scr, pltpu.VMEM(cells, bf16)],
        (at, got, x, sg, forward_t),
        6,
        1,
        after=last,
    )
    grad_parts = [grads[0]] + [hop("ch", d, grads[d]) for d in range(1, n_ch)]
    w_shapes = [array(f32, *first_weight.shape)] * 2 + [array(f32, 1, 2 * sz.chans)]
    if eight:
        block = call(bind(block_kernel), array(bf16, piece, width), [], (own, got_far), 0, after=(grads[0],))
        near = [hop("sp", 2 * d, block) for d in range(1, parts)]
        far_own = hop("sp", 1, block)
        small_shape = array(bf16, small_rows, width)
        small = call(bind(block_kernel), small_shape, [], (small, small_got), 0)
        small_got = hop("sp", 2, small)
        stacked = call(
            bind(stack_kernel), array(bf16, parts - 1, piece, width), [], near, 0, after=(*grad_parts[1:], small_got, far_own)
        )
        far = hop("sp", 1, stacked)
        small = call(bind(block_kernel), small_shape, [], (small, small_got), 0)
        in_grad, out_grad, w1_grad, w2_grad, b1_grad = call(
            bind(place_kernel),
            [array(bf16, width, hid), array(bf16, hid, width)] + w_shapes,
            [pltpu.VMEM((small_rows, width), f32)],
            (at, small, hop("sp", 4, small), far, far_own, block, *near),
            0,
            1,
        )
    else:
        high = (ch_at // 2 == 1)
        b_full = b_whole(b_keep, b_send, sp_at)
        in_grad = a_keep + hop("ch", 2, a_send).astype(f32)
        out_keep = jnp.where(high, b_full[1], b_full[0])
        out_grad = out_keep + hop("ch", 2, jnp.where(high, b_full[0], b_full[1]))
        small = call(bind(small_kernel), array(f32, small_rows, width), [], smalls, 0)
        in_grad, out_grad, small = lax.psum((in_grad, out_grad, small), "sp")
        half = width // 2
        in_grad = jnp.concatenate([in_grad[:, :half], in_grad[:, half:]], axis=0).astype(bf16)
        out_grad = out_grad.astype(bf16)
        w1_grad, w2_grad, b1_grad = call(bind(spread_small), w_shapes, [], (small,), 0)
    grad = call(bind(join_kernel), array(bf16, n_ch * sz.own, *cells[2:]), [], (at, *grad_parts), 0, 1)
    return (grad[: sz.rows], w1_grad, b1_grad.reshape(first_bias.shape), w2_grad, in_grad, out_grad)


def solution(mesh):
    placed = (
        P("sp", None, "ch"),
        P("sp", None, "ch"),
        P(None, "ch", None, None),
        P(None, "ch", None),
        P(None, "ch", None, None),
        P(None, "ch"),
        P("ch", None),
    )
    return jax.shard_map(
        local,
        mesh=mesh,
        in_specs=placed,
        out_specs=(
            P("sp", None, "ch"),
            P(None, "ch", None, None),
            P(None, "ch", None),
            P(None, "ch", None, None),
            P(None, "ch"),
            P("ch", None),
        ),
        check_vma=False,
    )
```

```python
import math

import jax
import jax.numpy as jnp
import ml_dtypes
import numpy as np
from jax import lax
from jax.experimental import pallas as pl
from jax.experimental.pallas import tpu as pltpu
from jax.sharding import PartitionSpec as P

LAT = 90
BAND_MAX = 16
LANES = 128
HALF = 64

eps = 1e-05
f32 = jnp.float32
bf16 = jnp.bfloat16
HIGH = lax.Precision.HIGH
VMEM_BYTES = 50 * 2**20


def up_to(value, step):
    return (value + step - 1) // step * step


class Sizes:
    def __init__(self, block, n_sp, n_ch):
        self.rows, self.lon, self.chans = block
        self.n_sp, self.n_ch = n_sp, n_ch
        self.width = self.chans * n_ch
        self.own = -(-self.rows // n_ch)
        self.bands = min(BAND_MAX, n_sp)
        self.samples = n_sp // self.bands
        self.modes = -(-(self.lon // 2 + 1) // n_sp)
        self.all_modes = self.modes * n_sp
        self.parts = 2 * self.chans // LANES
        self.pad = up_to(self.parts * self.own * self.modes, 16)
        self.sources = self.bands * n_ch
        self.lat_in = self.own * self.sources
        self.lat_modes = up_to(LAT, 16)
        self.planes = self.samples * self.modes
        self.lon_pad = up_to(self.lon, 16)

    def slot(self, q, r, m):
        return (q * self.own + r) * self.modes + m


def lon_tables(sz):
    mode = (np.arange(sz.n_sp)[None, :] * sz.modes + np.arange(sz.modes)[:, None]).reshape(-1, 1)
    cell = np.arange(sz.lon)[None, :]
    phase = 2.0 * np.pi / sz.lon * (mode * cell % sz.lon)
    live = (mode <= sz.lon // 2).astype(np.float64)
    inner = ((mode > 0) & (mode < sz.lon // 2)).astype(np.float64)
    scale = 1.0 / math.sqrt(sz.lon)
    cosine = np.cos(phase) * live * scale
    sine = np.sin(phase) * inner * scale
    forward = np.concatenate([cosine, -sine], axis=0)
    inverse = np.concatenate([cosine * (live + inner), -2.0 * sine], axis=0).T
    return forward.astype(np.float32), np.ascontiguousarray(inverse).astype(np.float32)


def lat_table(sz):
    r = np.arange(sz.own)[:, None, None]
    band = np.arange(sz.bands)[None, :, None]
    c = np.arange(sz.n_ch)[None, None, :]
    cell = band * sz.rows + c * sz.own + r
    live = np.logical_and(c * sz.own + r < sz.rows, cell < LAT).reshape(1, -1)
    cell = cell.reshape(1, -1)
    mode = np.arange(sz.lat_modes)[:, None]
    live = np.logical_and(live, mode < LAT) / math.sqrt(LAT)
    phase = 2.0 * np.pi / LAT * (mode * cell % LAT)
    return (
        (np.cos(phase) * live).astype(np.float32),
        (np.sin(phase) * live).astype(np.float32),
    )


def gelu(v):
    return v * (0.5 * (1.0 + lax.erf(v * np.float32(math.sqrt(0.5)))))


def gelu_pair(v):
    cdf = 0.5 * (1.0 + lax.erf(v * np.float32(math.sqrt(0.5))))
    pdf = jnp.exp(-0.5 * v * v) * np.float32(1.0 / math.sqrt(2.0 * math.pi))
    return v * cdf, cdf + v * pdf


def mm(a, b, precision=HIGH):
    return jnp.dot(a, b, precision=precision, preferred_element_type=f32)


def two_terms(table, rows):
    table = np.pad(table, ((0, rows - table.shape[0]), (0, 0)))
    first = table.astype(ml_dtypes.bfloat16)
    second = (table - first.astype(np.float32)).astype(ml_dtypes.bfloat16)
    return jnp.asarray(np.concatenate([first, second], axis=0))


def mm_two(table, values):
    y = jnp.dot(table, values.astype(bf16), preferred_element_type=f32)
    n = table.shape[0] // 2
    return y[:n] + y[n:]


def swap(values):
    lane = lax.broadcasted_iota(jnp.int32, values.shape, 1)
    turned = pltpu.roll(values, HALF, 1)
    return jnp.where(lane < HALF, turned, -turned)


def store_modes(sz, scr, y, r, c):
    n = sz.all_modes
    re, im = y[:n], y[n:]
    pieces = (re[:, :LANES], im[:, :LANES], re[:, LANES:] + pltpu.roll(im[:, LANES:], HALF, 1))
    for q, piece in enumerate(pieces):
        for m in range(sz.modes):
            scr[pl.ds(c * sz.pad + sz.slot(q, r, m), sz.n_sp, stride=sz.n_ch * sz.pad), :] = piece[
                m * sz.n_sp : (m + 1) * sz.n_sp
            ]


def load_modes(sz, scr, r, c):
    q0, q1, q2 = (
        jnp.concatenate(
            [
                scr[pl.ds(c * sz.pad + sz.slot(q, r, m), sz.n_sp, stride=sz.n_ch * sz.pad), :]
                for m in range(sz.modes)
            ],
            axis=0,
        )
        for q in range(3)
    )
    left = jnp.concatenate([q0, q1], axis=0)
    right = jnp.concatenate([q2, pltpu.roll(q2, HALF, 1)], axis=0)
    return jnp.concatenate([left, right], axis=1)


def wide(values):
    rows, lanes = values.shape
    return jnp.concatenate([values, jnp.zeros((rows, up_to(lanes, LANES) - lanes), f32)], axis=1)


def plane_start(sz, s, q, r, m):
    return s * sz.sources * sz.pad + sz.slot(q, r, m)


def center_scale(chunks, width):
    mean = sum(jnp.sum(v, axis=-1, keepdims=True) for v in chunks) / width
    chunks = [v - mean for v in chunks]
    var = sum(jnp.sum(v * v, axis=-1, keepdims=True) for v in chunks) / width
    recip = lax.rsqrt(var + eps)
    return [v * recip for v in chunks], recip


def norm_back(normed, recip, incoming, width):
    first = sum(jnp.sum(g, axis=-1, keepdims=True) for g in incoming) / width
    second = sum(jnp.sum(g * z, axis=-1, keepdims=True) for g, z in zip(incoming, normed)) / width
    return [recip * (g - first - z * second) for g, z in zip(incoming, normed)]


def gather_parts(sz, at_ref, own_ref, parts, out_ref):
    me = at_ref[4]
    for r in range(sz.own):
        out_ref[me, r] = own_ref[me * sz.own + r]
    for d, part in enumerate(parts):
        out_ref[me ^ (d + 1)] = part[...]


def norm_spectrum_kernel(sz, at_ref, *refs):
    own_ref, *parts = refs[: sz.n_ch]
    tab_ref, out_ref, x_ref, scr = refs[sz.n_ch :]
    gather_parts(sz, at_ref, own_ref, parts, x_ref)
    for r in range(sz.own):
        normed, _ = center_scale([x_ref[c, r].astype(f32) for c in range(sz.n_ch)], sz.width)
        for c in range(sz.n_ch):
            store_modes(sz, scr, mm(tab_ref[...], wide(normed[c])), r, c)
    out_ref[...] = scr[...].astype(bf16)


def lat_forward(sz, scr, cs, p):
    s, m = divmod(p, sz.modes)
    x0, x1, x2 = (
        jnp.concatenate(
            [
                scr[pl.ds(plane_start(sz, s, q, r, m), sz.sources, stride=sz.pad), :]
                for r in range(sz.own)
            ],
            axis=0,
        )
        for q in range(3)
    )
    both = jnp.concatenate(
        [jnp.concatenate([x0, x1, x2], axis=1), jnp.concatenate([x1, -x0, swap(x2)], axis=1)], axis=0
    )
    return mm_two(cs, both)


def lat_inverse(sz, scr, cs_t, o, p):
    s, m = divmod(p, sz.modes)
    o0, o1, o2 = (o[:, q * LANES : (q + 1) * LANES] for q in range(3))
    both = jnp.concatenate(
        [jnp.concatenate([o0, o1, o2], axis=1), jnp.concatenate([-o1, o0, -swap(o2)], axis=1)], axis=0
    )
    y = mm_two(cs_t, both)
    for q in range(3):
        for r in range(sz.own):
            scr[pl.ds(plane_start(sz, s, q, r, m), sz.sources, stride=sz.pad), :] = y[
                r * sz.sources : (r + 1) * sz.sources, q * LANES : (q + 1) * LANES
            ]


def mix_kernel(sz, in_ref, cs_ref, cst_ref, w1_ref, b1_ref, w2_ref, out_ref, scr, spec, mixed):
    n = sz.lat_modes
    scr[...] = in_ref[...].astype(f32)
    for p in range(sz.planes):
        spec[p * n : (p + 1) * n, :] = lat_forward(sz, scr, cs_ref[...], p)

    def block(i, carry):
        rows = pl.ds(pl.multiple_of(i * 2 * n, 16), 2 * n)
        mixed[rows, :] = mm(gelu(mm(spec[rows, :], w1_ref[...]) + b1_ref[...]), w2_ref[...])
        return carry

    lax.fori_loop(0, sz.planes // 2, block, 0)
    for p in range(sz.planes):
        lat_inverse(sz, scr, cst_ref[...], mixed[p * n : (p + 1) * n, :], p)
    out_ref[...] = scr[...].astype(bf16)


def mix_save_kernel(sz, in_ref, cs_ref, w1_ref, b1_ref, spec_ref, act_ref, slope_ref, scr):
    n = sz.lat_modes
    scr[...] = in_ref[...].astype(f32)
    for p in range(sz.planes):
        spec_ref[p * n : (p + 1) * n, :] = lat_forward(sz, scr, cs_ref[...], p)

    def block(i, carry):
        rows = pl.ds(pl.multiple_of(i * 2 * n, 16), 2 * n)
        act, slope = gelu_pair(mm(spec_ref[rows, :], w1_ref[...]) + b1_ref[...])
        act_ref[rows, :] = act
        slope_ref[rows, :] = slope
        return carry

    lax.fori_loop(0, sz.planes // 2, block, 0)


def mix_back_kernel(sz, in_ref, cs_ref, w2t_ref, slope_ref, dmix_ref, dpre_ref, scr):
    n = sz.lat_modes
    scr[...] = in_ref[...].astype(f32)
    for p in range(sz.planes):
        dmix_ref[p * n : (p + 1) * n, :] = lat_forward(sz, scr, cs_ref[...], p)

    def block(i, carry):
        rows = pl.ds(pl.multiple_of(i * 2 * n, 16), 2 * n)
        dpre_ref[rows, :] = mm(dmix_ref[rows, :], w2t_ref[...]) * slope_ref[rows, :]
        return carry

    lax.fori_loop(0, sz.planes // 2, block, 0)


def spectrum_back_cut_kernel(sz, at_ref, dpre_ref, cst_ref, w1t_ref, *refs):
    near_cut_kernel(sz, at_ref, *refs[:4], *refs[5:7], refs[9])
    spectrum_back_kernel(sz, dpre_ref, cst_ref, w1t_ref, refs[4], *refs[7:9])


def spectrum_back_kernel(sz, dpre_ref, cst_ref, w1t_ref, out_ref, scr, dspec):
    n = sz.lat_modes

    def block(i, carry):
        rows = pl.ds(pl.multiple_of(i * 2 * n, 16), 2 * n)
        dspec[rows, :] = mm(dpre_ref[rows, :], w1t_ref[...])
        return carry

    lax.fori_loop(0, sz.planes // 2, block, 0)
    for p in range(sz.planes):
        lat_inverse(sz, scr, cst_ref[...], dspec[p * n : (p + 1) * n, :], p)
    out_ref[...] = scr[...].astype(bf16)


def mlp_kernel(sz, at_ref, in_ref, x_ref, inv_ref, invt_ref, *refs):
    n = sz.n_ch
    own_ref, *parts = refs[:n]
    win_refs, wout_refs = refs[n : 2 * n], refs[2 * n : 3 * n]
    out_ref, sg_ref, mid_ref, upf_ref, act_ref, hg_ref, part_ref, scr, z_scr, mg_scr, rs_scr, up_ref, act_scr, hg_scr = refs[3 * n :]
    me, first_row = at_ref[4], at_ref[5]
    gather_parts(sz, at_ref, own_ref, parts, up_ref)
    for r in range(sz.own):

        def mask(r=r):
            for c in range(n):
                up_ref[c, r] = jnp.zeros((sz.lon, sz.chans), bf16)

        pl.when(first_row + r >= LAT)(mask)
    scr[...] = in_ref[...].astype(f32)
    mid_ref[...] = jnp.zeros(mid_ref.shape, bf16)
    upf_ref[...] = jnp.zeros(upf_ref.shape, bf16)
    c_all = range(sz.n_ch)

    def place(r, c):
        return (slice(r * sz.lon_pad, r * sz.lon_pad + sz.lon), slice(c * sz.chans, (c + 1) * sz.chans))

    for r in range(sz.own):
        xs = [x_ref[c, r].astype(f32) for c in c_all]
        normed, _ = center_scale(xs, sz.width)
        summed = [
            xs[c] + normed[c] + mm_two(inv_ref[...], load_modes(sz, scr, r, c))[: sz.lon, : sz.chans] for c in c_all
        ]
        zs, recip = center_scale(summed, sz.width)
        rs_scr[r] = jnp.broadcast_to(recip, (sz.lon, LANES))
        for c in c_all:
            z_scr[c, r] = zs[c]
            mid_ref[place(r, c)] = zs[c].astype(bf16)
            upf_ref[place(r, c)] = up_ref[c, r]
    mg_scr[...] = jnp.zeros(mg_scr.shape, f32)
    nt = (((1,), (1,)), ((), ()))

    for d in range(n):
        k = at_ref[1] ^ (d // 2)
        pre = mm(mid_ref[...], win_refs[d][...], None)
        back = lax.dot_general(upf_ref[...], wout_refs[d][...], nt, preferred_element_type=f32)
        act, slope = gelu_pair(pre)
        grad = (back * slope).astype(bf16)
        mg_scr[...] += lax.dot_general(grad, win_refs[d][...], nt, preferred_element_type=f32)
        if d % 2:
            act_scr[...] = act.astype(bf16)
            hg_scr[...] = grad
            dense_parts(sz, part_ref, k, mid_ref, upf_ref, act_scr, hg_scr)
        else:
            act_ref[k] = act.astype(bf16)
            hg_ref[k] = grad
    for r in range(sz.own):
        zs = [z_scr[c, r] for c in c_all]
        grads = norm_back(zs, rs_scr[r][:, :1], [mg_scr[place(r, c)] for c in c_all], sz.width)
        for c in c_all:
            total = up_ref[c, r].astype(f32) + grads[c]
            sg_ref[c, r] = total
            store_modes(sz, scr, mm(invt_ref[...], wide(total)), r, c)
    out_ref[...] = scr[...].astype(bf16)


def field_kernel(sz, at_ref, in_ref, x_ref, sg_ref, fwdt_ref, *refs):
    outs, (scr, out_scr) = refs[: sz.n_ch], refs[sz.n_ch :]
    scr[...] = in_ref[...].astype(f32)
    c_all = range(sz.n_ch)
    for r in range(sz.own):
        normed, recip = center_scale([x_ref[c, r].astype(f32) for c in c_all], sz.width)
        sg = [sg_ref[c, r] for c in c_all]
        incoming = [sg[c] + mm_two(fwdt_ref[...], load_modes(sz, scr, r, c))[: sz.lon, : sz.chans] for c in c_all]
        grads = norm_back(normed, recip, incoming, sz.width)
        for c in c_all:
            out_scr[c, r] = (sg[c] + grads[c]).astype(bf16)
    for d, out in enumerate(outs):
        out[...] = out_scr[at_ref[4] ^ d]


def join_kernel(sz, at_ref, *refs):
    parts, out_ref = refs[:-1], refs[-1]
    for d, part in enumerate(parts):
        for r in range(sz.own):
            out_ref[(at_ref[4] ^ d) * sz.own + r] = part[r]


def dense_keep_kernel(sz, at_ref, mid_ref, upf_ref, act_ref, hg_ref, got_ref,
                      a_keep, a_send, b_keep, b_send, scr):
    high, x = at_ref[1], at_ref[2]
    tn = (((0,), (0,)), ((), ()))
    half = sz.width // 2
    for k, out in ((high, a_keep), (1 - high, a_send)):
        for side in range(2):
            lanes = slice(side * half, (side + 1) * half)
            part = lax.dot_general(mid_ref[:, lanes], hg_ref[k], tn, preferred_element_type=f32)
            out[:, lanes] = (part + got_ref[k, 0, :, lanes].astype(f32)).astype(out.dtype)
    rows = scr.shape[0] // 2
    for k in range(2):
        part = lax.dot_general(act_ref[k], upf_ref[...], tn, preferred_element_type=f32)
        scr[...] = part + got_ref[k, 1].astype(f32)
        b_keep[k] = scr[pl.ds(pl.multiple_of(x * rows, 16), rows), :]
        b_send[k] = scr[pl.ds(pl.multiple_of((1 - x) * rows, 16), rows), :].astype(bf16)


def lane_runs(p, b, size):
    if b == 0:
        return [(p * LANES, p * LANES + size)]
    return [(p * LANES + size, (p + 1) * LANES), (2 * LANES + p * HALF, 2 * LANES + (p + 1) * HALF)]


def take(values, p, b, size, axis):
    pieces = [lax.slice_in_dim(values, i, j, axis=axis) for i, j in lane_runs(p, b, size)]
    return pieces[0] if len(pieces) == 1 else jnp.concatenate(pieces, axis=axis)


def dense_step_kernel(sz, at_ref, a_keep, a_got, b_keep, b_got, a2_keep, a2_send, b2_keep, b2_send, scr):
    high, x = at_ref[1], at_ref[2]
    rows = a2_keep.shape[0]
    scr[...] = a_keep[...] + a_got[...].astype(f32)
    a2_keep[...] = scr[pl.ds(pl.multiple_of(x * rows, 16), rows), :]
    a2_send[...] = scr[pl.ds(pl.multiple_of((1 - x) * rows, 16), rows), :].astype(bf16)
    b2_keep[...] = b_keep[high] + b_got[high].astype(f32)
    b2_send[...] = (b_keep[1 - high] + b_got[1 - high].astype(f32)).astype(bf16)


def near_cut_kernel(sz, at_ref, a_keep, a_got, b_keep, b_got, keep, send, cut):
    low = at_ref[3] % 2
    many = cut.shape[1] // 2
    for p in range(cut.shape[0]):
        rows = slice(p * many, (p + 1) * many)
        cut[p, 0:many] = a_keep[rows, :] + a_got[rows, :].astype(f32)
        cut[p, many : 2 * many] = b_keep[rows, :] + b_got[rows, :].astype(f32)
    for h in range(2):
        keep[h] = cut[2 * h + low]
        send[h] = cut[2 * h + 1 - low].astype(bf16)


def far_cut_kernel(sz, at_ref, keep, got, own, send):
    high = at_ref[3] // 2
    own[...] = keep[high] + got[high].astype(f32)
    send[...] = (keep[1 - high] + got[1 - high].astype(f32)).astype(bf16)


def stack_kernel(sz, *refs):
    for i, ref in enumerate(refs[:-1]):
        refs[-1][i] = ref[...]


def block_kernel(sz, own, *refs):
    parts, out_ref = refs[:-1], refs[-1]
    total = own[...].astype(f32)
    for part in parts:
        total = total + part[...].astype(f32)
    out_ref[...] = total.astype(bf16)


def small_kernel(sz, spec_ref, dpre_ref, act_ref, dmix_ref, out_ref):
    tn = (((0,), (0,)), ((), ()))
    size = sz.chans // 2
    out_ref[...] = jnp.zeros(out_ref.shape, f32)
    for g, (left, right) in enumerate(((spec_ref, dpre_ref), (act_ref, dmix_ref))):
        big = lax.dot_general(left[...], right[...], tn, precision=HIGH, preferred_element_type=f32)
        for b in range(2):
            rows = [take(big, p, b, size, 0) for p in range(2)]
            real = take(rows[0], 0, b, size, 1) + take(rows[1], 1, b, size, 1)
            imag = take(rows[0], 1, b, size, 1) - take(rows[1], 0, b, size, 1)
            for p, value in enumerate((real, imag)):
                k = (g * 2 + p) * 2 + b
                out_ref[0:size, k * size : (k + 1) * size] = value
    bias = jnp.sum(dpre_ref[...], axis=0, keepdims=True)
    for p in range(2):
        for b in range(2):
            k = p * 2 + b
            out_ref[size : size + 1, k * size : (k + 1) * size] = take(bias, p, b, size, 1)


def small_round_kernel(sz, *refs):
    out_ref, scr = refs[4:]
    small_kernel(sz, *refs[:4], scr)
    out_ref[...] = scr[...].astype(bf16)


def place_kernel(sz, at_ref, s_own, s_far, far, far_own, *refs):
    parts = sz.n_sp // 2
    near, (in_ref, out_ref, w1_ref, w2_ref, b1_ref, scr) = refs[:parts], refs[parts:]
    many = far.shape[1] // 2
    half = sz.width // 2
    x = at_ref[2]
    for i in range(2 * parts):
        ref = near[i] if i < parts else far_own if i == parts else far.at[i - parts - 1]
        place = (x ^ (i // parts)) * parts + (at_ref[3] ^ (i % parts))
        base = pl.multiple_of(place * many, 16)
        in_ref[pl.ds(base, many), :] = ref[0:many, 0:half]
        in_ref[pl.ds(base + half, many), :] = ref[0:many, half : 2 * half]
        out_ref[pl.ds(base, many), :] = ref[many:, :]
    scr[...] = s_own[...].astype(f32) + s_far[...].astype(f32)
    spread_small(sz, scr, w1_ref, w2_ref, b1_ref)


def spread_small(sz, scr, w1_ref, w2_ref, b1_ref):
    size = sz.chans // 2
    for g, out in enumerate((w1_ref, w2_ref)):
        for p in range(2):
            for b in range(2):
                k = (g * 2 + p) * 2 + b
                out[p, b] = scr[0:size, k * size : (k + 1) * size]
    for p in range(2):
        for b in range(2):
            k = p * 2 + b
            b1_ref[p, b : b + 1, :] = scr[size : size + 1, k * size : (k + 1) * size]


def call(body, outs, scratch, args, micros, scalars=0, after=()):
    in_specs = [pl.BlockSpec(memory_space=pltpu.SMEM)] * scalars
    in_specs += [pl.BlockSpec(memory_space=pltpu.VMEM)] * (len(args) - scalars)
    in_specs += [pl.BlockSpec(memory_space=pl.ANY)] * len(after)
    n_args, n_after = len(args), len(after)

    def wrapped(*refs):
        body(*refs[:n_args], *refs[n_args + n_after :])

    return pl.pallas_call(
        wrapped,
        in_specs=in_specs,
        out_shape=outs,
        scratch_shapes=scratch,
        compiler_params=pltpu.CompilerParams(vmem_limit_bytes=VMEM_BYTES),
        cost_estimate=pl.CostEstimate(flops=micros * 10**9, bytes_accessed=2**20, transcendentals=0),
    )(*args, *after)


def block_diagonal(weight):
    blocks, size = weight.shape[0], weight.shape[1]
    ident = jnp.eye(blocks, dtype=f32)
    return jnp.einsum("be,bio->bieo", ident, weight).reshape(blocks * size, blocks * size)


def lane_order(values, axis, chans):
    def cut(a, b):
        return lax.slice_in_dim(values, a, b, axis=axis)
    return jnp.concatenate(
        [cut(0, LANES), cut(chans, chans + LANES), cut(LANES, chans), cut(chans + LANES, 2 * chans)], axis=axis
    )


def natural_order(values, axis, chans):
    def cut(a, b):
        return lax.slice_in_dim(values, a, b, axis=axis)
    rest = chans - LANES
    return jnp.concatenate(
        [cut(0, LANES), cut(2 * LANES, 2 * LANES + rest), cut(LANES, 2 * LANES), cut(2 * LANES + rest, 2 * chans)],
        axis=axis,
    )


def big_weight(weight):
    real, imag = block_diagonal(weight[0]), block_diagonal(weight[1])
    full = jnp.concatenate(
        [jnp.concatenate([real, imag], axis=1), jnp.concatenate([-imag, real], axis=1)], axis=0
    )
    chans = real.shape[0]
    return lane_order(lane_order(full, 0, chans), 1, chans)


def small_grad(big, blocks):
    chans = big.shape[0] // 2
    size = chans // blocks
    full = natural_order(natural_order(big, 0, chans), 1, chans)
    full = full.reshape(2, blocks, size, 2, blocks, size)
    diag = jnp.stack([full[:, b, :, :, b, :] for b in range(blocks)], axis=0)
    real = diag[:, 0, :, 0] + diag[:, 1, :, 1]
    imag = diag[:, 0, :, 1] - diag[:, 1, :, 0]
    return jnp.stack([real, imag], axis=0)


def hop(axis, distance, values):
    n = lax.axis_size(axis)
    return lax.ppermute(values, axis, [(i, i ^ distance) for i in range(n)])


def dense_parts(sz, out_ref, k, mid_ref, upf_ref, act_ref, hg_ref):
    tn = (((0,), (0,)), ((), ()))
    half = sz.width // 2
    for side in range(2):
        lanes = slice(side * half, (side + 1) * half)
        out_ref[k, 0, :, lanes] = lax.dot_general(
            mid_ref[:, lanes], hg_ref[...], tn, preferred_element_type=f32
        ).astype(out_ref.dtype)
    out_ref[k, 1] = lax.dot_general(act_ref[...], upf_ref[...], tn, preferred_element_type=f32).astype(out_ref.dtype)


def b_whole(keep, send, sp_at):
    odd = sp_at % 2 == 1
    send = send.astype(f32)
    return jnp.concatenate([jnp.where(odd, send, keep), jnp.where(odd, keep, send)], axis=1)


def array(dtype, *shape):
    return jax.ShapeDtypeStruct(shape, dtype)


def split(*shape):
    return array(f32, *shape), array(bf16, *shape)


def local(field, cotangent, first_weight, first_bias, second_weight, dense_in, dense_out):
    n_sp, n_ch = lax.axis_size("sp"), lax.axis_size("ch")
    sz = Sizes(field.shape, n_sp, n_ch)
    both = ("sp", "ch")
    hid, width = dense_in.shape[1], sz.width
    forward, inverse = lon_tables(sz)
    forward_t, inverse_2 = two_terms(forward.T, sz.lon_pad), two_terms(inverse, sz.lon_pad)
    forward, inverse_t = jnp.asarray(forward), jnp.asarray(inverse.T)
    cosine, sine = lat_table(sz)
    cs = two_terms(np.concatenate([cosine, sine], axis=1), sz.lat_modes)
    cs_t = two_terms(np.concatenate([cosine.T, sine.T], axis=1), sz.lat_in)
    sp_at, ch_at = lax.axis_index("sp"), lax.axis_index("ch")
    first_row = sp_at % sz.bands * sz.rows + ch_at * sz.own
    at = jnp.stack([ch_at % 2, ch_at // 2, sp_at % 2, sp_at // 2, ch_at, first_row]).astype(jnp.int32)
    extra = sz.own * n_ch - sz.rows
    if extra:
        field, cotangent = (jnp.pad(v, ((0, extra), (0, 0), (0, 0))) for v in (field, cotangent))

    def row_parts(values):
        got = {}
        for d in reversed(range(1, n_ch)):
            got[d] = hop("ch", d, lax.dynamic_slice_in_dim(values, (ch_at ^ d) * sz.own, sz.own, 0))
        return [got[d] for d in range(1, n_ch)]

    def swap_modes(message):
        message = message.reshape(n_sp * n_ch, sz.pad, LANES)
        message = lax.all_to_all(message, both, split_axis=0, concat_axis=0, tiled=True)
        return message.reshape(n_sp * n_ch * sz.pad, LANES)

    def bind(kernel):
        return lambda *refs: kernel(sz, *refs)

    message = array(bf16, n_sp * n_ch * sz.pad, LANES)
    scr = pltpu.VMEM(message.shape, f32)
    flat = array(f32, sz.planes * sz.lat_modes, 2 * sz.chans)
    flat_scr = pltpu.VMEM(flat.shape, f32)
    cells = (n_ch, sz.own, sz.lon, sz.chans)

    x_parts = row_parts(field)
    x_parts, cotangent, dense_in, dense_out = lax.optimization_barrier((x_parts, cotangent, dense_in, dense_out))
    sent, x = call(
        bind(norm_spectrum_kernel), (message, array(bf16, *cells)), [scr], (at, field, *x_parts, forward), 3, 1
    )
    up_parts = row_parts(cotangent)
    far_in, far_out = hop("ch", 2, dense_in), hop("ch", 2, dense_out)
    near_in, near_out = hop("ch", 1, dense_in), hop("ch", 1, dense_out)
    sent, first_weight, second_weight, first_bias = lax.optimization_barrier(
        (sent, first_weight, second_weight, first_bias)
    )
    w1, w2 = big_weight(first_weight), big_weight(second_weight)
    b1 = lane_order(first_bias.reshape(1, -1), 1, sz.chans)
    got = swap_modes(sent)
    modes_in = got
    sent = call(
        bind(mix_kernel),
        message,
        [scr, flat_scr, flat_scr],
        (modes_in, cs, cs_t, w1, b1, w2),
        10,
        after=(far_in, far_out),
    )
    got = swap_modes(sent)
    spec, act, slope = call(
        bind(mix_save_kernel), (flat, flat, flat), [scr], (modes_in, cs, w1, b1), 30, after=(sent,)
    )
    wins = (dense_in, near_in, far_in, hop("ch", 1, far_in))
    wouts = (dense_out, near_out, far_out, hop("ch", 1, far_out))
    tokens = sz.own * sz.lon_pad
    grown = array(bf16, tokens, width)
    hidden = array(bf16, n_ch // 2, tokens, hid)
    sent, sg, mid, upf, hidden_act, hidden_grad, sent_part = call(
        bind(mlp_kernel),
        (message, array(f32, *cells), grown, grown, hidden, hidden, array(bf16, n_ch // 2, 2, hid, width)),
        [
            scr,
            pltpu.VMEM(cells, f32),
            pltpu.VMEM(grown.shape, f32),
            pltpu.VMEM((sz.own, sz.lon, LANES), f32),
            pltpu.VMEM(cells, bf16),
            pltpu.VMEM(hidden.shape[1:], bf16),
            pltpu.VMEM(hidden.shape[1:], bf16),
        ],
        (at, got, x, inverse_2, inverse_t, cotangent, *up_parts, *wins, *wouts),
        20,
        1,
        after=(slope,),
    )
    got = swap_modes(sent)
    factors = (at, mid, upf, hidden_act, hidden_grad)
    got_part = hop("ch", 1, sent_part)
    a_keep, a_send, b_keep, b_send = call(
        bind(dense_keep_kernel),
        split(hid, width) + split(2, hid // 2, width),
        [pltpu.VMEM((hid, width), f32)],
        (*factors, got_part),
        0,
        1,
    )
    eight = n_sp == 8
    small_rows = up_to(sz.chans // 2 + 1, 16)
    before = (a_keep,)
    if eight:
        a_got, b_got = hop("ch", 2, a_send), hop("sp", 1, b_send)
        a_keep, a_send, b_keep, b_send = before = call(
            bind(dense_step_kernel),
            split(hid // 2, width) * 2,
            [pltpu.VMEM((hid, width), f32)],
            (at, a_keep, a_got, b_keep, b_got),
            0,
            1,
        )
        a_got, b_got = hop("sp", 1, a_send), hop("ch", 2, b_send)
    dmix, dpre = call(
        bind(mix_back_kernel), (flat, flat), [scr], (got, cs, w2.T, slope), 6, after=before[:1]
    )
    parts = n_sp // 2
    piece = 2 * hid // n_sp
    back_args = (dpre, cs_t, w1.T)
    if eight:
        sent, keep, send = call(
            bind(spectrum_back_cut_kernel),
            (message,) + split(2, piece, width),
            [scr, flat_scr, pltpu.VMEM((parts, piece, width), f32)],
            (at, *back_args, a_keep, a_got, b_keep, b_got),
            6,
            1,
        )
        got_near = hop("sp", 2, send)
    else:
        sent = call(bind(spectrum_back_kernel), message, [scr, flat_scr], back_args, 6)
    got = swap_modes(sent)
    last = ()
    smalls = (spec, dpre, act, dmix)
    if eight:
        small = call(
            bind(small_round_kernel),
            array(bf16, small_rows, width),
            [pltpu.VMEM((small_rows, width), f32)],
            smalls,
            0,
            after=(keep,),
        )
        small_got = hop("sp", 1, small)
        own, send = call(bind(far_cut_kernel), split(piece, width), [], (at, keep, got_near), 0, 1)
        got_far = hop("sp", 4, send)
        last = (own, small_got)
    grads = call(
        bind(field_kernel),
        [array(bf16, *cells[1:])] * n_ch,
        [scr, pltpu.VMEM(cells, bf16)],
        (at, got, x, sg, forward_t),
        6,
        1,
        after=last,
    )
    grad_parts = [grads[0]] + [hop("ch", d, grads[d]) for d in range(1, n_ch)]
    w_shapes = [array(f32, *first_weight.shape)] * 2 + [array(f32, *first_bias.shape)]
    if eight:
        block = call(bind(block_kernel), array(bf16, piece, width), [], (own, got_far), 0, after=(grads[0],))
        near = [hop("sp", 2 * d, block) for d in range(1, parts)]
        far_own = hop("sp", 1, block)
        small_shape = array(bf16, small_rows, width)
        small = call(bind(block_kernel), small_shape, [], (small, small_got), 0)
        small_got = hop("sp", 2, small)
        stacked = call(
            bind(stack_kernel), array(bf16, parts - 1, piece, width), [], near, 0, after=(*grad_parts[1:], small_got, far_own)
        )
        far = hop("sp", 1, stacked)
        small = call(bind(block_kernel), small_shape, [], (small, small_got), 0)
        in_grad, out_grad, w1_grad, w2_grad, b1_grad = call(
            bind(place_kernel),
            [array(bf16, width, hid), array(bf16, hid, width)] + w_shapes,
            [pltpu.VMEM((small_rows, width), f32)],
            (at, small, hop("sp", 4, small), far, far_own, block, *near),
            0,
            1,
        )
    else:
        high = (ch_at // 2 == 1)
        b_full = b_whole(b_keep, b_send, sp_at)
        in_grad = a_keep + hop("ch", 2, a_send).astype(f32)
        out_keep = jnp.where(high, b_full[1], b_full[0])
        out_grad = out_keep + hop("ch", 2, jnp.where(high, b_full[0], b_full[1]))
        small = call(bind(small_kernel), array(f32, small_rows, width), [], smalls, 0)
        in_grad, out_grad, small = lax.psum((in_grad, out_grad, small), "sp")
        half = width // 2
        in_grad = jnp.concatenate([in_grad[:, :half], in_grad[:, half:]], axis=0).astype(bf16)
        out_grad = out_grad.astype(bf16)
        w1_grad, w2_grad, b1_grad = call(bind(spread_small), w_shapes, [], (small,), 0)
    grad = call(bind(join_kernel), array(bf16, n_ch * sz.own, *cells[2:]), [], (at, *grad_parts), 0, 1)
    return (grad[: sz.rows], w1_grad, b1_grad, w2_grad, in_grad, out_grad)


def solution(mesh):
    placed = (
        P("sp", None, "ch"),
        P("sp", None, "ch"),
        P(None, "ch", None, None),
        P(None, "ch", None),
        P(None, "ch", None, None),
        P(None, "ch"),
        P("ch", None),
    )
    return jax.shard_map(
        local,
        mesh=mesh,
        in_specs=placed,
        out_specs=(
            P("sp", None, "ch"),
            P(None, "ch", None, None),
            P(None, "ch", None),
            P(None, "ch", None, None),
            P(None, "ch"),
            P("ch", None),
        ),
        check_vma=False,
    )
```
